512 devices in a mesh: seq: 128 (over z_hi, y, x, core), kvh: 4 (over z_lo).
Axes of the slice: x: 4, y: 8, z: 8 (z_hi: 2, z_lo: 4; z = z_hi * 4 + z_lo), core: 2. Of those that a mesh axis runs over, the one named last changes fastest.
Arguments:
- queries: bfloat16 [65536, 4096], P('seq', 'kvh'), may hold values from -120 to 120
- keys: bfloat16 [65536, 1024], P('seq', 'kvh'), may hold values from -4 to 4
- values: bfloat16 [65536, 1024], P('seq', 'kvh'), may hold values from -6 to 6
- episode_lengths: int32 [64], replicated, may hold values from 1 to 2048, 65536 in all
Outputs:
- attended: bfloat16 [65536, 4096], P(('seq', 'kvh'))
The draws below stay inside these ranges and needn't reach their ends.
Inputs may be any that keep to these rules, and one draw needn't show every extreme that they name: `episode_lengths`: 64 whole episodes that fill the 65536 tokens; the longest has exactly 2048 tokens.
All inputs are finite; a program needn't handle non-finite values.
Results may differ from the reference program's by a relative error of at most 0.0039.
Values may be sent and summed in bfloat16 or wider, within the bound.
A program may use at most 64 MiB of HBM per device.

```python
import math
import jax
import jax.numpy as jnp
import numpy as np
from jax import lax

HEADS = 32
KV_HEADS = 8
HEAD = 128
TOK_DEV = 512
GROUP = 4
WINDOW = 1536
TOKENS = 65536
EPISODES = 64
LONGEST = 2048
N_SEQ = 128


def shared_keys(key):
    sampled = jax.random.normal(key, (TOKENS, KV_HEADS * HEAD), jnp.float32)
    return jnp.clip(sampled, -4.0, 4.0)


def draw_keys(key, part):
    sampled = shared_keys(key)
    return sampled.astype(jnp.bfloat16)


def draw_queries(key, part):
    key = jax.random.fold_in(key, 5)
    return jax.random.normal(key, (TOKENS, HEADS * HEAD), jnp.float32).astype(jnp.bfloat16)


def steps_of(key, extent, shards, least, high):
    level, own = 1.0, jax.random.fold_in(key, 6)
    for axis_at, shards_of in shards:
        draws = jnp.exp(jax.random.uniform(jax.random.fold_in(own, axis_at), (shards_of,), jnp.float32, least / len(shards), high / len(shards)))
        level = level * jnp.repeat(draws, extent[axis_at] // shards_of).reshape([-1 if axis == axis_at else 1 for axis in range(len(extent))])
    return level


def split_up(number_of, total, most, lean):
    portions = [(1 << 20) // math.isqrt(standing ** lean) + 1 for standing in range(2, number_of + 1)]
    spare, given = total - most - (number_of - 1), [1] * (number_of - 1)
    while spare > 0:
        candidates = [i for i in range(number_of - 1) if given[i] < most]
        mass, remaining = sum([portions[i] for i in candidates]), spare
        for i in candidates:
            extra = min(most - given[i], max(1, remaining * portions[i] // mass), spare)
            given[i] = given[i] + extra
            spare = spare - extra
    return np.array([most] + given)


def ragged_sizes(key, amount, total, most, skew):
    if amount == 2:
        one = jax.random.randint(key, (), max(1, total - most), min(most, total - 1) + 1)
        return jnp.stack([one, total - one])
    sizes = jnp.asarray(split_up(amount, total, most, skew), jnp.int32)
    pairs = (amount - 1) // 2
    giver, taker = sizes[1:1 + 2 * pairs:2], sizes[2:2 + 2 * pairs:2]
    room = jnp.minimum(giver - 1, most - taker)
    shifted = jax.random.randint(jax.random.fold_in(key, 1), (pairs,), 0, 1 << 20) % (room + 1)
    sizes = sizes.at[1:1 + 2 * pairs:2].set(giver - shifted).at[2:2 + 2 * pairs:2].set(taker + shifted)
    return sizes[jax.random.permutation(jax.random.fold_in(key, 2), amount)]


def gaussian(own_key, dims, spread, most, cuts=(), held_as=jnp.bfloat16):
    drawn = spread * jax.random.normal(own_key, dims, jnp.float32)
    if cuts:
        drawn = drawn * steps_of(own_key, dims, cuts, -0.22, 0.18)
    return jnp.clip(drawn, -most, most).astype(held_as)


def setup_inputs(seed: int = 0) -> dict:
    key_list = jax.random.split(jax.random.key(seed), 5)
    queries = draw_queries(jax.random.fold_in(key_list[4], 71), 0)
    keys = draw_keys(jax.random.fold_in(key_list[4], 71), 0)
    values = gaussian(key_list[2], (TOKENS, KV_HEADS * HEAD), 1.0, 6.0, ((0, 128), (1, 4)))
    episode_lengths = ragged_sizes(key_list[3], EPISODES, TOKENS, LONGEST, 2).astype(jnp.int32)
    return dict(queries=queries, keys=keys, values=values, episode_lengths=episode_lengths)


def episode_index(positions, episode_ends):
    return lax.optimization_barrier(jnp.sum((episode_ends[None, :] <= positions[:, None]).astype(jnp.int32), axis=1))

def reference(queries, keys, values, episode_lengths):
    episode_ends = jnp.cumsum(episode_lengths).astype(jnp.int32)
    score_scale = 1.0 / math.sqrt(HEAD)
    padded_keys = jnp.pad(keys, ((WINDOW, 0), (0, 0)))
    padded_values = jnp.pad(values, ((WINDOW, 0), (0, 0)))
    key_count = WINDOW + TOK_DEV

    def one_block(block_index):
        first_row = block_index * TOK_DEV
        query_block = lax.dynamic_slice_in_dim(queries, first_row, TOK_DEV, 0).astype(jnp.float32)
        query_block = query_block.reshape(TOK_DEV, KV_HEADS, GROUP, HEAD)
        key_block = lax.dynamic_slice_in_dim(padded_keys, first_row, key_count, 0).astype(jnp.float32)
        key_block = key_block.reshape(key_count, KV_HEADS, HEAD)
        value_block = lax.dynamic_slice_in_dim(padded_values, first_row, key_count, 0).astype(jnp.float32)
        value_block = value_block.reshape(key_count, KV_HEADS, HEAD)
        query_position = first_row + jnp.arange(TOK_DEV, dtype=jnp.int32)
        key_position = first_row - WINDOW + jnp.arange(key_count, dtype=jnp.int32)
        distance = query_position[:, None] - key_position[None, :]
        same_episode = episode_index(query_position, episode_ends)[:, None] == episode_index(key_position, episode_ends)[None, :]
        visible = (distance >= 0) & (distance < WINDOW) & (key_position[None, :] >= 0) & same_episode
        scores = jnp.einsum('tgjd,kgd->gjtk', query_block, key_block) * score_scale
        scores = jnp.where(visible[None, None], scores, -jnp.inf)
        row_max = lax.optimization_barrier(jnp.max(scores, axis=-1, keepdims=True))
        weights = jnp.exp(scores - row_max)
        row_total = lax.optimization_barrier(jnp.sum(weights, axis=-1))
        weights_low = lax.optimization_barrier(weights.astype(jnp.bfloat16)).astype(jnp.float32)
        summed = jnp.einsum('gjtk,kgd->tgjd', weights_low, value_block)
        result = summed / jnp.transpose(row_total, (2, 0, 1))[..., None]
        return result.reshape(TOK_DEV, HEADS * HEAD).astype(jnp.bfloat16)
    blocks_out = lax.map(one_block, jnp.arange(N_SEQ, dtype=jnp.int32))
    return blocks_out.reshape(TOKENS, HEADS * HEAD)
```

```python
import functools
import math

import jax
import jax.numpy as jnp
from jax import lax
from jax.experimental import pallas as pl
from jax.experimental.pallas import tpu as pltpu
from jax.sharding import PartitionSpec as P

HEAD = 128
GROUP = 4
WINDOW = 1536
MESH = pl.DeviceIdType.MESH
MASKED = -1e30


def attend(q, kv_ref, base, begin, scale, stack=2):
    rows = begin.shape[0]
    row = lax.broadcasted_iota(jnp.int32, (rows, rows), 0)
    col = lax.broadcasted_iota(jnp.int32, (rows, rows), 1)
    last = col <= row
    edge_seen = jnp.where(last, col + WINDOW, col) >= begin
    middle_seen = lax.broadcasted_iota(jnp.int32, (rows, WINDOW - rows), 1) + rows >= begin
    last, edge_seen, middle_seen = (
        jnp.concatenate([mask] * stack, 0) for mask in (last, edge_seen, middle_seen)
    )

    def part(offset, count):
        span = pl.ds(base + offset, count)
        return kv_ref[span, 0:HEAD], kv_ref[span, HEAD:2 * HEAD]

    first_k, first_v = part(0, rows)
    middle_k, middle_v = part(rows, WINDOW - rows)
    last_k, last_v = part(WINDOW, rows)

    def score(lhs, keys):
        return lax.dot_general(
            lhs, keys, (((1,), (1,)), ((), ())), preferred_element_type=jnp.float32
        )

    def add_up(weights, values):
        return jnp.dot(weights, values, preferred_element_type=jnp.float32)

    outs = []
    for j in range(0, GROUP, stack):
        lhs = jnp.concatenate(q[j:j + stack], 0)
        edge = jnp.where(last, score(lhs, last_k), score(lhs, first_k))
        edge = jnp.where(edge_seen, edge, MASKED)
        middle = jnp.where(middle_seen, score(lhs, middle_k), MASKED)
        top = jnp.maximum(
            jnp.max(middle, axis=1, keepdims=True), jnp.max(edge, axis=1, keepdims=True)
        )
        edge = jnp.exp2((edge - top) * scale)
        middle = jnp.exp2((middle - top) * scale)
        total = jnp.sum(middle, axis=1, keepdims=True) + jnp.sum(edge, axis=1, keepdims=True)
        edge = edge.astype(jnp.bfloat16)
        none = jnp.zeros_like(edge)
        summed = add_up(middle.astype(jnp.bfloat16), middle_v)
        summed += add_up(jnp.where(last, edge, none), last_v)
        summed += add_up(jnp.where(last, none, edge), first_v)
        out = (summed / total).astype(jnp.bfloat16)
        outs += [out[i * rows:(i + 1) * rows] for i in range(stack)]
    return outs


def kernel(
    n_chips, n_kvh, ends_ref, q_hbm, k_hbm, v_hbm, out_hbm,
    q_ref, kv0_ref, kv1_ref, start_ref, stage_ref,
    load_sem, kv_send, kv_recv, out_send, out_recv, own_sem,
):
    block = k_hbm.shape[0]
    rows = block // n_kvh
    episodes = ends_ref.shape[0]
    seq = lax.axis_index("seq")
    kvh = lax.axis_index("kvh")
    chip = seq // 2
    first = lax.rem(seq, 2) == 0
    second = lax.rem(seq, 2) == 1
    scale = math.log2(math.e) / math.sqrt(HEAD)

    kv_refs = (kv0_ref, kv1_ref)

    def slot(g, i):
        return kv_refs[g].at[pl.ds(i * block, block)]

    own = []
    for g in range(2):
        for i, src in enumerate((k_hbm, v_hbm)):
            own.append(pltpu.make_async_copy(
                src.at[:, pl.ds(g * HEAD, HEAD)],
                kv_refs[g].at[pl.ds(3 * block, block), pl.ds(i * HEAD, HEAD)],
                load_sem.at[2 * g + i],
            ))
    own_q = []
    for g in range(2):
        for j in range(GROUP):
            own_q.append(pltpu.make_async_copy(
                q_hbm.at[:, pl.ds((g * GROUP + j) * HEAD, HEAD)],
                q_ref.at[g, j],
                load_sem.at[4 + g * GROUP + j],
            ))
    for copy in own + own_q:
        copy.start()

    barrier = pltpu.get_barrier_semaphore()

    def greet(s, k):
        pl.semaphore_signal(barrier, inc=1, device_id=(s, k), device_id_type=MESH)

    for step in range(1, n_kvh):
        greet(seq, lax.rem(kvh + step, n_kvh))

    @pl.when(first)
    def _():
        @pl.when(chip >= 1)
        def _():
            greet(seq - 2, kvh)
            greet(seq - 1, kvh)

        @pl.when(chip >= 2)
        def _():
            greet(seq - 3, kvh)

    @pl.when(second)
    def _():
        greet(seq - 1, kvh)

    @pl.when(seq < 2 * n_chips - 3)
    def _():
        pl.semaphore_wait(barrier, n_kvh + 1)

    @pl.when((seq == 2 * n_chips - 3) | (seq == 2 * n_chips - 2))
    def _():
        pl.semaphore_wait(barrier, n_kvh)

    @pl.when(seq == 2 * n_chips - 1)
    def _():
        pl.semaphore_wait(barrier, n_kvh - 1)

    def send(g, here, there, by, sem):
        return pltpu.make_async_remote_copy(
            src_ref=slot(g, here), dst_ref=slot(g, there),
            send_sem=kv_send.at[g, sem], recv_sem=kv_recv.at[g, there],
            device_id=(seq + by, kvh), device_id_type=MESH,
        )

    def arrived(g, there):
        send(g, there, there, 1, 0).wait_recv()

    for copy in own:
        copy.wait()

    @pl.when(first)
    def _():
        for g in range(2):
            @pl.when(chip < n_chips - 1)
            def _():
                send(g, 3, 1, 2, 0).start()
            send(g, 3, 2, 1, 1).start()

    @pl.when(second)
    def _():
        for g in range(2):
            @pl.when(chip < n_chips - 1)
            def _():
                send(g, 3, 2, 1, 0).start()

            @pl.when(chip < n_chips - 2)
            def _():
                send(g, 3, 0, 3, 1).start()

    @pl.when(first & (chip == 0))
    def _():
        for ref in kv_refs:
            ref[0:3 * block, :] = jnp.zeros((3 * block, 2 * HEAD), jnp.bfloat16)

    @pl.when(first & (chip == 1))
    def _():
        for ref in kv_refs:
            ref[0:block, :] = jnp.zeros((block, 2 * HEAD), jnp.bfloat16)

    position = seq * block + lax.broadcasted_iota(jnp.int32, (block, HEAD), 0)
    start_ref[...] = jnp.zeros((block, HEAD), jnp.int32)

    def add_episode(e, end):
        end = end + ends_ref[e]
        start_ref[...] = jnp.where(position >= end, end, start_ref[...])
        return end

    lax.fori_loop(0, episodes, add_episode, jnp.int32(0))
    for copy in own_q:
        copy.wait()

    def pass_on(g):
        @pl.when(chip >= 1)
        def _():
            arrived(g, 2)
        send(g, 2, 1, 1, 2).start()

        @pl.when(chip >= 1)
        def _():
            arrived(g, 1)
        send(g, 1, 0, 1, 3).start()

    def window_in(g):
        @pl.when(first & (chip >= 2))
        def _():
            arrived(g, 0)

        @pl.when(second)
        def _():
            for i in range(3):
                arrived(g, i)

    def out_copy(u, g, r):
        return pltpu.make_async_remote_copy(
            src_ref=stage_ref.at[u],
            dst_ref=out_hbm.at[:, pl.ds(pl.multiple_of((kvh * 2 + g) * GROUP * HEAD, HEAD), GROUP * HEAD)],
            send_sem=out_send.at[u], recv_sem=out_recv.at[g, kvh],
            device_id=(seq, r), device_id_type=MESH,
        )

    def own_copy(u, g):
        return pltpu.make_async_copy(
            stage_ref.at[u],
            out_hbm.at[:, pl.ds(pl.multiple_of((kvh * 2 + g) * GROUP * HEAD, HEAD), GROUP * HEAD)],
            own_sem.at[g],
        )

    def target(step):
        late, odd = step // 2, step % 2
        half, low = kvh // 2, kvh % 2
        far = (1 - half) * (3 - odd) + half * odd
        near = 2 * half + (1 - low) * (1 - odd) + low * odd
        return (1 - late) * far + late * near

    def unit(g, step):
        r = target(step)
        u = 4 * g + step
        base = pl.multiple_of(r * rows, rows)
        begin = start_ref[pl.ds(base, rows), 0:1] - (seq * block - WINDOW + base)
        q = [q_ref[g, j, pl.ds(base, rows), :] for j in range(GROUP)]
        outs = attend(q, kv_refs[g], base, begin, scale)
        for j in range(GROUP):
            stage_ref[u, :, j * HEAD:(j + 1) * HEAD] = outs[j]

        @pl.when(step < 3)
        def _():
            out_copy(u, g, r).start()

        @pl.when(step == 3)
        def _():
            own_copy(u, g).start()

    @pl.when(first)
    def _():
        pass_on(0)

    window_in(0)

    @pl.loop(0, 4)
    def _(step):
        @pl.when(first & (step == 1))
        def _():
            pass_on(1)

        unit(0, step)

    window_in(1)

    @pl.loop(0, 4)
    def _(step):
        unit(1, step)

    @pl.when(first)
    def _():
        for g in range(2):
            @pl.when(chip < n_chips - 1)
            def _():
                send(g, 3, 1, 2, 0).wait_send()
            for sem in range(1, 4):
                send(g, 3, 2, 1, sem).wait_send()

    @pl.when(second)
    def _():
        for g in range(2):
            @pl.when(chip < n_chips - 1)
            def _():
                send(g, 3, 2, 1, 0).wait_send()

            @pl.when(chip < n_chips - 2)
            def _():
                send(g, 3, 0, 3, 1).wait_send()

    for g in range(2):
        for step in range(3):
            out_copy(4 * g + step, g, kvh).wait_send()
        own_copy(4 * g + 3, g).wait()
        for step in range(1, n_kvh):
            source = lax.rem(kvh + step, n_kvh)
            pltpu.make_async_remote_copy(
                src_ref=stage_ref.at[0],
                dst_ref=out_hbm.at[:, pl.ds(pl.multiple_of((source * 2 + g) * GROUP * HEAD, HEAD), GROUP * HEAD)],
                send_sem=out_send.at[0], recv_sem=out_recv.at[g, source],
                device_id=(seq, source), device_id_type=MESH,
            ).wait_recv()


def body(n_chips, n_kvh, queries, keys, values, episode_lengths):
    block = keys.shape[0]
    rows = block // n_kvh
    width = queries.shape[1]
    anywhere = pl.BlockSpec(memory_space=pl.ANY)
    return pl.pallas_call(
        functools.partial(kernel, n_chips, n_kvh),
        out_shape=jax.ShapeDtypeStruct((rows, width * n_kvh), jnp.bfloat16),
        in_specs=[pl.BlockSpec(memory_space=pltpu.SMEM), anywhere, anywhere, anywhere],
        out_specs=anywhere,
        scratch_shapes=[
            pltpu.VMEM((2, GROUP, block, HEAD), jnp.bfloat16),
            pltpu.VMEM((4 * block, 2 * HEAD), jnp.bfloat16),
            pltpu.VMEM((4 * block, 2 * HEAD), jnp.bfloat16),
            pltpu.VMEM((block, HEAD), jnp.int32),
            pltpu.VMEM((8, rows, GROUP * HEAD), jnp.bfloat16),
            pltpu.SemaphoreType.DMA((12,)),
            pltpu.SemaphoreType.DMA((2, 4)),
            pltpu.SemaphoreType.DMA((2, 3)),
            pltpu.SemaphoreType.DMA((8,)),
            pltpu.SemaphoreType.DMA((2, n_kvh)),
            pltpu.SemaphoreType.DMA((2,)),
        ],
        compiler_params=pltpu.CompilerParams(
            collective_id=0, has_side_effects=True, vmem_limit_bytes=48 << 20
        ),
        name="attention",
    )(episode_lengths, queries, keys, values)


def solution(mesh):
    return jax.shard_map(
        functools.partial(body, mesh.shape["seq"] // 2, mesh.shape["kvh"]),
        mesh=mesh,
        in_specs=(P("seq", "kvh"), P("seq", "kvh"), P("seq", "kvh"), P()),
        out_specs=P(("seq", "kvh"), None),
        check_vma=False,
    )
```

```python
import functools
import math

import jax
import jax.numpy as jnp
from jax import lax
from jax.experimental import pallas as pl
from jax.experimental.pallas import tpu as pltpu
from jax.sharding import PartitionSpec as P

HEAD = 128
GROUP = 4
WINDOW = 1536
MESH = pl.DeviceIdType.MESH
MASKED = -1e30
STACK = 2


def attend(q, kv_ref, base, begin, scale, finish):
    stack = STACK
    rows = begin.shape[0]
    row = lax.broadcasted_iota(jnp.int32, (rows, rows), 0)
    col = lax.broadcasted_iota(jnp.int32, (rows, rows), 1)
    last = col <= row
    edge_seen = jnp.where(last, col + WINDOW, col) >= begin
    middle_seen = lax.broadcasted_iota(jnp.int32, (rows, WINDOW - rows), 1) + rows >= begin
    last, edge_seen, middle_seen = (
        jnp.concatenate([mask] * stack, 0) for mask in (last, edge_seen, middle_seen)
    )

    def part(offset, count):
        span = pl.ds(base + offset, count)
        return kv_ref[span, 0:HEAD], kv_ref[span, HEAD:2 * HEAD]

    first_k, first_v = part(0, rows)
    middle_k, middle_v = part(rows, WINDOW - rows)
    last_k, last_v = part(WINDOW, rows)

    def score(lhs, keys):
        return lax.dot_general(
            lhs, keys, (((1,), (1,)), ((), ())), preferred_element_type=jnp.float32
        )

    def add_up(weights, values):
        return jnp.dot(weights, values, preferred_element_type=jnp.float32)

    for j in range(0, GROUP, stack):
        lhs = jnp.concatenate(q[j:j + stack], 0)
        edge = jnp.where(last, score(lhs, last_k), score(lhs, first_k))
        edge = jnp.where(edge_seen, edge, MASKED)
        middle = jnp.where(middle_seen, score(lhs, middle_k), MASKED)
        top = jnp.maximum(
            jnp.max(middle, axis=1, keepdims=True), jnp.max(edge, axis=1, keepdims=True)
        )
        edge = jnp.exp2((edge - top) * scale)
        middle = jnp.exp2((middle - top) * scale)
        total = jnp.sum(middle, axis=1, keepdims=True) + jnp.sum(edge, axis=1, keepdims=True)
        edge = edge.astype(jnp.bfloat16)
        none = jnp.zeros_like(edge)
        summed = add_up(middle.astype(jnp.bfloat16), middle_v)
        summed += add_up(jnp.where(last, edge, none), last_v)
        summed += add_up(jnp.where(last, none, edge), first_v)
        out = (summed / total).astype(jnp.bfloat16)
        finish(j // stack, [out[i * rows:(i + 1) * rows] for i in range(stack)])


def kernel(
    n_chips, n_kvh, lengths_hbm, q_hbm, k_hbm, v_hbm, out_ref,
    lengths_ref, q_ref, kv0_ref, kv1_ref, relay_ref, start_ref, stage_ref,
    load_sem, kv_send, kv_recv, relay_recv, out_send, out_recv, own_sem,
):
    block = k_hbm.shape[0]
    rows = block // n_kvh
    wide = STACK * HEAD
    pieces = GROUP // STACK
    episodes = lengths_ref.shape[0]
    seq = lax.axis_index("seq")
    kvh = lax.axis_index("kvh")
    chip = seq // 2
    first = lax.rem(seq, 2) == 0
    second = lax.rem(seq, 2) == 1
    n_seq = 2 * n_chips
    half = n_chips
    relay = n_seq - 2
    scale = math.log2(math.e) / math.sqrt(HEAD)
    kv_refs = (kv0_ref, kv1_ref)

    def slot(g, i):
        return kv_refs[g].at[pl.ds(i * block, block)]

    own = []
    for g in range(2):
        for i, src in enumerate((k_hbm, v_hbm)):
            own.append(pltpu.make_async_copy(
                src.at[:, pl.ds(g * HEAD, HEAD)],
                kv_refs[g].at[pl.ds(3 * block, block), pl.ds(i * HEAD, HEAD)],
                load_sem.at[2 * g + i],
            ))
    later = [pltpu.make_async_copy(lengths_hbm, lengths_ref, load_sem.at[4])]
    for g in range(2):
        for j in range(GROUP):
            later.append(pltpu.make_async_copy(
                q_hbm.at[:, pl.ds((g * GROUP + j) * HEAD, HEAD)],
                q_ref.at[g, j],
                load_sem.at[5 + g * GROUP + j],
            ))
    for copy in own + later:
        copy.start()

    barrier = pltpu.get_barrier_semaphore()

    def greet(s, k):
        pl.semaphore_signal(barrier, inc=1, device_id=(s, k), device_id_type=MESH)

    for step in range(1, n_kvh):
        greet(seq, lax.rem(kvh + step, n_kvh))

    @pl.when(first)
    def _():
        @pl.when(chip >= 1)
        def _():
            greet(seq - 1, kvh)

        @pl.when((chip >= 1) & (seq != half))
        def _():
            greet(seq - 2, kvh)

        @pl.when((chip >= 2) & (seq != half + 2))
        def _():
            greet(seq - 3, kvh)

        @pl.when(seq == half)
        def _():
            greet(relay, kvh)

        @pl.when(seq == relay)
        def _():
            greet(half - 2, kvh)

    @pl.when(second)
    def _():
        greet(seq - 1, kvh)

    four = (seq == n_seq - 3) | (seq == half - 1)

    @pl.when((seq < n_seq - 1) & jnp.logical_not(four))
    def _():
        pl.semaphore_wait(barrier, n_kvh + 1)

    @pl.when(four)
    def _():
        pl.semaphore_wait(barrier, n_kvh)

    @pl.when(seq == n_seq - 1)
    def _():
        pl.semaphore_wait(barrier, n_kvh - 1)

    def send(g, src, dst, to, sem, recv):
        return pltpu.make_async_remote_copy(
            src_ref=src, dst_ref=dst, send_sem=kv_send.at[g, sem], recv_sem=recv,
            device_id=(to, kvh), device_id_type=MESH,
        )

    def pass_slot(g, here, there, by, sem):
        return send(g, slot(g, here), slot(g, there), seq + by, sem, kv_recv.at[g, there])

    def arrived(g, there):
        pass_slot(g, there, there, 1, 0).wait_recv()

    has_next = (chip < n_chips - 1) & (seq != half - 2)
    has_second = (chip < n_chips - 2) & (seq != half - 1)

    def to_relay(g):
        return send(g, slot(g, 3), relay_ref.at[g], relay, 0, relay_recv.at[g])

    def from_relay(g):
        return send(g, relay_ref.at[g], slot(g, 1), half, 0, kv_recv.at[g, 1])

    def to_sibling(g):
        return pass_slot(g, 3, 2, 1, 1)

    def to_second(g):
        return pass_slot(g, 3, 0, 3, 1)

    def ahead_even(g):
        @pl.when(has_next)
        def _():
            pass_slot(g, 3, 1, 2, 0).start()

        @pl.when(seq == half - 2)
        def _():
            to_relay(g).start()
        to_sibling(g).start()

    def ahead_odd(g):
        @pl.when(chip < n_chips - 1)
        def _():
            pass_slot(g, 3, 2, 1, 0).start()

    def ahead_second(g):
        @pl.when(has_second)
        def _():
            to_second(g).start()

    def pass_on(g):
        @pl.when(seq == relay)
        def _():
            to_relay(g).wait_recv()
            from_relay(g).start()

        @pl.when(chip >= 1)
        def _():
            arrived(g, 2)
        pass_slot(g, 2, 1, 1, 2).start()

        @pl.when(seq == half)
        def _():
            pass_slot(g, 2, 0, 2, 4).start()

        @pl.when(chip >= 1)
        def _():
            arrived(g, 1)
        pass_slot(g, 1, 0, 1, 3).start()

    def window_in(g):
        @pl.when(first & (chip >= 2))
        def _():
            arrived(g, 0)

        @pl.when(second)
        def _():
            for i in range(3):
                arrived(g, i)

    for copy in own:
        copy.wait()

    @pl.when(first)
    def _():
        ahead_even(0)

    @pl.when(second)
    def _():
        ahead_odd(0)

    @pl.when(first & (chip == 0))
    def _():
        for ref in kv_refs:
            ref[0:3 * block, :] = jnp.zeros((3 * block, 2 * HEAD), jnp.bfloat16)

    @pl.when(first & (chip == 1))
    def _():
        for ref in kv_refs:
            ref[0:block, :] = jnp.zeros((block, 2 * HEAD), jnp.bfloat16)

    for copy in later:
        copy.wait()
    position = seq * block + lax.broadcasted_iota(jnp.int32, (block, HEAD), 0)
    start_ref[...] = jnp.zeros((block, HEAD), jnp.int32)

    def add_episode(e, end):
        end = end + lengths_ref[e]
        start_ref[...] = jnp.where(position >= end, end, start_ref[...])
        return end

    lax.fori_loop(0, episodes, add_episode, jnp.int32(0))

    def out_columns(k, g, piece):
        return pl.ds(pl.multiple_of(((k * 2 + g) * GROUP + piece * STACK) * HEAD, HEAD), wide)

    def staged(u, piece):
        return stage_ref.at[u, :, pl.ds(piece * wide, wide)]

    def out_copy(u, g, piece, to, source):
        return pltpu.make_async_remote_copy(
            src_ref=staged(u, piece), dst_ref=out_ref.at[:, out_columns(source, g, piece)],
            send_sem=out_send.at[u, piece], recv_sem=out_recv.at[g, source, piece],
            device_id=(seq, to), device_id_type=MESH,
        )

    def own_copy(u, g, piece):
        return pltpu.make_async_copy(
            staged(u, piece), out_ref.at[:, out_columns(kvh, g, piece)], own_sem.at[g, piece]
        )

    def target(step):
        late, odd = step // 2, step % 2
        upper, low = kvh // 2, kvh % 2
        far = (1 - upper) * (3 - odd) + upper * odd
        near = 2 * upper + (1 - low) * (1 - odd) + low * odd
        return (1 - late) * far + late * near

    def unit(g, step):
        r = target(step)
        u = 4 * g + step
        base = pl.multiple_of(r * rows, rows)
        begin = start_ref[pl.ds(base, rows), 0:1] - (seq * block - WINDOW + base)
        q = [q_ref[g, j, pl.ds(base, rows), :] for j in range(GROUP)]

        def finish(piece, outs):
            for j in range(STACK):
                at = (piece * STACK + j) * HEAD
                stage_ref[u, :, at:at + HEAD] = outs[j]

            @pl.when(step < 3)
            def _():
                out_copy(u, g, piece, r, kvh).start()

            @pl.when(step == 3)
            def _():
                own_copy(u, g, piece).start()

        attend(q, kv_refs[g], base, begin, scale, finish)

    @pl.when(first)
    def _():
        pass_on(0)
        ahead_even(1)

    @pl.when(second)
    def _():
        @pl.when(chip < n_chips - 1)
        def _():
            pass_slot(0, 3, 2, 1, 0).wait_send()
        ahead_second(0)

    window_in(0)

    @pl.when(second)
    def _():
        ahead_odd(1)

    @pl.loop(0, 4)
    def _(step):
        @pl.when(first & (step == 1))
        def _():
            pass_on(1)

        @pl.when(second & (step == 1))
        def _():
            ahead_second(1)

        unit(0, step)

    window_in(1)

    @pl.loop(0, 4)
    def _(step):
        unit(1, step)

    @pl.when(first)
    def _():
        for g in range(2):
            @pl.when(has_next | (seq == half - 2))
            def _():
                pass_slot(g, 3, 1, 2, 0).wait_send()

            @pl.when(seq == relay)
            def _():
                from_relay(g).wait_send()

            @pl.when(seq == half)
            def _():
                pass_slot(g, 2, 0, 2, 4).wait_send()
            for sem in range(1, 4):
                pass_slot(g, 3, 2, 1, sem).wait_send()

    @pl.when(second)
    def _():
        @pl.when(chip < n_chips - 1)
        def _():
            pass_slot(1, 3, 2, 1, 0).wait_send()
        for g in range(2):
            @pl.when(has_second)
            def _():
                to_second(g).wait_send()

    for g in range(2):
        for piece in range(pieces):
            for step in range(3):
                out_copy(4 * g + step, g, piece, kvh, kvh).wait_send()
            own_copy(4 * g + 3, g, piece).wait()
            for step in range(1, n_kvh):
                source = lax.rem(kvh + step, n_kvh)
                out_copy(0, g, piece, source, source).wait_recv()


def body(n_chips, n_kvh, queries, keys, values, episode_lengths):
    block = keys.shape[0]
    rows = block // n_kvh
    width = queries.shape[1]
    hbm = pl.BlockSpec(memory_space=pltpu.HBM)
    return pl.pallas_call(
        functools.partial(kernel, n_chips, n_kvh),
        out_shape=jax.ShapeDtypeStruct((rows, width * n_kvh), jnp.bfloat16),
        in_specs=[hbm, hbm, hbm, hbm],
        out_specs=pl.BlockSpec(memory_space=pl.ANY),
        scratch_shapes=[
            pltpu.SMEM(episode_lengths.shape, jnp.int32),
            pltpu.VMEM((2, GROUP, block, HEAD), jnp.bfloat16),
            pltpu.VMEM((4 * block, 2 * HEAD), jnp.bfloat16),
            pltpu.VMEM((4 * block, 2 * HEAD), jnp.bfloat16),
            pltpu.VMEM((2, block, 2 * HEAD), jnp.bfloat16),
            pltpu.VMEM((block, HEAD), jnp.int32),
            pltpu.VMEM((8, rows, GROUP * HEAD), jnp.bfloat16),
            pltpu.SemaphoreType.DMA((13,)),
            pltpu.SemaphoreType.DMA((2, 5)),
            pltpu.SemaphoreType.DMA((2, 3)),
            pltpu.SemaphoreType.DMA((2,)),
            pltpu.SemaphoreType.DMA((8, GROUP // STACK)),
            pltpu.SemaphoreType.DMA((2, n_kvh, GROUP // STACK)),
            pltpu.SemaphoreType.DMA((2, GROUP // STACK)),
        ],
        compiler_params=pltpu.CompilerParams(
            collective_id=0, has_side_effects=True, vmem_limit_bytes=60 << 20
        ),
        name="attention",
    )(episode_lengths, queries, keys, values)


def solution(mesh):
    return jax.shard_map(
        functools.partial(body, mesh.shape["seq"] // 2, mesh.shape["kvh"]),
        mesh=mesh,
        in_specs=(P("seq", "kvh"), P("seq", "kvh"), P("seq", "kvh"), P()),
        out_specs=P(("seq", "kvh"), None),
        check_vma=False,
    )
```

```python
import functools
import math

import jax
import jax.numpy as jnp
from jax import lax
from jax.experimental import pallas as pl
from jax.experimental.pallas import tpu as pltpu
from jax.sharding import PartitionSpec as P

HEAD = 128
GROUP = 4
WINDOW = 1536
MESH = pl.DeviceIdType.MESH
MASKED = -1e30
STACK = 2


def attend(q, kv_ref, base, begin, scale, finish):
    stack = STACK
    rows = begin.shape[0]
    row = lax.broadcasted_iota(jnp.int32, (rows, rows), 0)
    col = lax.broadcasted_iota(jnp.int32, (rows, rows), 1)
    last = col <= row
    edge_seen = jnp.where(last, col + WINDOW, col) >= begin
    middle_seen = lax.broadcasted_iota(jnp.int32, (rows, WINDOW - rows), 1) + rows >= begin
    last, edge_seen, middle_seen = (
        jnp.concatenate([mask] * stack, 0) for mask in (last, edge_seen, middle_seen)
    )

    def part(offset, count):
        span = pl.ds(base + offset, count)
        return kv_ref[span, 0:HEAD], kv_ref[span, HEAD:2 * HEAD]

    first_k, first_v = part(0, rows)
    middle_k, middle_v = part(rows, WINDOW - rows)
    last_k, last_v = part(WINDOW, rows)

    def score(lhs, keys):
        return lax.dot_general(
            lhs, keys, (((1,), (1,)), ((), ())), preferred_element_type=jnp.float32
        )

    def add_up(weights, values):
        return jnp.dot(weights, values, preferred_element_type=jnp.float32)

    for j in range(0, GROUP, stack):
        lhs = jnp.concatenate(q[j:j + stack], 0)
        edge = jnp.where(last, score(lhs, last_k), score(lhs, first_k))
        edge = jnp.where(edge_seen, edge, MASKED)
        middle = jnp.where(middle_seen, score(lhs, middle_k), MASKED)
        top = jnp.maximum(
            jnp.max(middle, axis=1, keepdims=True), jnp.max(edge, axis=1, keepdims=True)
        )
        edge = jnp.exp2((edge - top) * scale)
        middle = jnp.exp2((middle - top) * scale)
        total = jnp.sum(middle, axis=1, keepdims=True) + jnp.sum(edge, axis=1, keepdims=True)
        edge = edge.astype(jnp.bfloat16)
        none = jnp.zeros_like(edge)
        summed = add_up(middle.astype(jnp.bfloat16), middle_v)
        summed += add_up(jnp.where(last, edge, none), last_v)
        summed += add_up(jnp.where(last, none, edge), first_v)
        out = (summed / total).astype(jnp.bfloat16)
        finish(j // stack, [out[i * rows:(i + 1) * rows] for i in range(stack)])


def crossing(n_seq):
    half = n_seq // 2
    if n_seq == 128:
        by = (119, 127, 79, 125)
    else:
        by = (n_seq - 5, n_seq - 1, n_seq - 7, n_seq - 3)
    return (
        (half - 1, 2, 0, None), (half - 1, 2, 1, by[0]),
        (half - 2, 1, 0, by[1]), (half - 2, 1, 1, by[2]),
        (half - 3, 0, 0, None), (half - 3, 0, 1, by[3]),
    )


def kernel(
    n_chips, n_kvh, lengths_hbm, q_hbm, k_hbm, v_hbm, out_ref,
    lengths_ref, q_ref, kv0_ref, kv1_ref, relay_ref, start_ref, stage_ref,
    load_sem, kv_send, kv_recv, relay_recv, out_send, out_recv, own_sem,
):
    block = k_hbm.shape[0]
    rows = block // n_kvh
    wide = STACK * HEAD
    pieces = GROUP // STACK
    episodes = lengths_ref.shape[0]
    seq = lax.axis_index("seq")
    kvh = lax.axis_index("kvh")
    chip = seq // 2
    first = lax.rem(seq, 2) == 0
    second = lax.rem(seq, 2) == 1
    n_seq = 2 * n_chips
    half = n_chips
    part = block // 2
    routes = crossing(n_seq)
    relays = [route for route in routes if route[3] is not None]
    scale = math.log2(math.e) / math.sqrt(HEAD)
    kv_refs = (kv0_ref, kv1_ref)

    def slot(g, i):
        return kv_refs[g].at[pl.ds(i * block, block)]

    own = []
    for g in range(2):
        for i, src in enumerate((k_hbm, v_hbm)):
            own.append(pltpu.make_async_copy(
                src.at[:, pl.ds(g * HEAD, HEAD)],
                kv_refs[g].at[pl.ds(3 * block, block), pl.ds(i * HEAD, HEAD)],
                load_sem.at[2 * g + i],
            ))
    later = [pltpu.make_async_copy(lengths_hbm, lengths_ref, load_sem.at[4])]
    for g in range(2):
        for j in range(GROUP):
            later.append(pltpu.make_async_copy(
                q_hbm.at[:, pl.ds((g * GROUP + j) * HEAD, HEAD)],
                q_ref.at[g, j],
                load_sem.at[5 + g * GROUP + j],
            ))
    for copy in own + later:
        copy.start()

    barrier = pltpu.get_barrier_semaphore()

    def greet(s, k):
        pl.semaphore_signal(barrier, inc=1, device_id=(s, k), device_id_type=MESH)

    for step in range(1, n_kvh):
        greet(seq, lax.rem(kvh + step, n_kvh))

    @pl.when(first)
    def _():
        @pl.when(chip >= 1)
        def _():
            greet(seq - 1, kvh)

        @pl.when((chip >= 1) & (seq != half))
        def _():
            greet(seq - 2, kvh)

        @pl.when((chip >= 2) & (seq != half + 2))
        def _():
            greet(seq - 3, kvh)

        @pl.when(seq == half)
        def _():
            for _, _, _, by in relays:
                greet(by, kvh)

    @pl.when(second)
    def _():
        greet(seq - 1, kvh)

    for source, _, _, by in relays:
        @pl.when(seq == by)
        def _():
            greet(source, kvh)

    more = (seq == half - 2) | (seq == half - 3)
    for _, _, _, by in relays:
        if by < n_seq - 4:
            more = more | (seq == by)

    @pl.when(more)
    def _():
        pl.semaphore_wait(barrier, n_kvh + 2)

    @pl.when((seq < n_seq - 2) & jnp.logical_not(more))
    def _():
        pl.semaphore_wait(barrier, n_kvh + 1)

    @pl.when(seq >= n_seq - 2)
    def _():
        pl.semaphore_wait(barrier, n_kvh)

    def send(g, src, dst, to, sem, recv):
        return pltpu.make_async_remote_copy(
            src_ref=src, dst_ref=dst, send_sem=kv_send.at[g, sem], recv_sem=recv,
            device_id=(to, kvh), device_id_type=MESH,
        )

    def pass_slot(g, here, there, by, sem):
        return send(g, slot(g, here), slot(g, there), seq + by, sem, kv_recv.at[g, there])

    def arrived(g, there):
        pass_slot(g, there, there, 1, 0).wait_recv()

    has_next = chip < n_chips - 1
    has_second = chip < n_chips - 2

    def to_sibling(g):
        return pass_slot(g, 3, 2, 1, 1)

    def to_second(g):
        return pass_slot(g, 3, 0, 3, 1)

    def rows_of(g, i, piece):
        return kv_refs[g].at[pl.ds(i * block + piece * part, part)]

    def to_relay(g, route, sem):
        source, there, piece, by = route
        return send(g, rows_of(g, 3, piece), relay_ref.at[g], by, sem, relay_recv.at[g])

    def from_relay(g, route):
        source, there, piece, by = route
        return send(g, relay_ref.at[g], rows_of(g, there, piece), half, 2, kv_recv.at[g, there])

    def cross(g, source, sem):
        for route in routes:
            if route[0] != source:
                continue
            if route[3] is None:
                there, piece = route[1:3]
                send(
                    g, rows_of(g, 3, piece), rows_of(g, there, piece), half, sem,
                    kv_recv.at[g, there],
                ).start()
            else:
                to_relay(g, route, sem).start()

    def ahead_even(g):
        @pl.when(has_next & (seq != half - 2))
        def _():
            pass_slot(g, 3, 1, 2, 0).start()
        to_sibling(g).start()

    def ahead_odd(g):
        @pl.when(has_next & (seq != half - 1))
        def _():
            pass_slot(g, 3, 2, 1, 0).start()

    def ahead_second(g):
        @pl.when(has_second & (seq != half - 1) & (seq != half - 3))
        def _():
            to_second(g).start()

    def relay(g):
        for route in relays:
            @pl.when(seq == route[3])
            def _():
                to_relay(g, route, 0).wait_recv()
                from_relay(g, route).start()

    def pass_on(g):
        @pl.when(chip >= 1)
        def _():
            arrived(g, 2)
        pass_slot(g, 2, 1, 1, 2).start()

        @pl.when(seq == half)
        def _():
            pass_slot(g, 2, 0, 2, 4).start()

        @pl.when(chip >= 1)
        def _():
            arrived(g, 1)
        pass_slot(g, 1, 0, 1, 3).start()

    def window_in(g):
        @pl.when(first & (chip >= 2))
        def _():
            arrived(g, 0)

        @pl.when(second)
        def _():
            for i in range(3):
                arrived(g, i)

    for copy in own:
        copy.wait()

    for source, sem in ((half - 2, 0), (half - 1, 0), (half - 3, 1)):
        @pl.when(seq == source)
        def _():
            cross(0, source, sem)

    @pl.when(first)
    def _():
        ahead_even(0)

    @pl.when(second)
    def _():
        ahead_odd(0)

    @pl.when(first & (chip == 0))
    def _():
        for ref in kv_refs:
            ref[0:3 * block, :] = jnp.zeros((3 * block, 2 * HEAD), jnp.bfloat16)

    @pl.when(first & (chip == 1))
    def _():
        for ref in kv_refs:
            ref[0:block, :] = jnp.zeros((block, 2 * HEAD), jnp.bfloat16)

    for copy in later:
        copy.wait()
    position = seq * block + lax.broadcasted_iota(jnp.int32, (block, HEAD), 0)
    start_ref[...] = jnp.zeros((block, HEAD), jnp.int32)

    def add_episode(e, end):
        end = end + lengths_ref[e]
        start_ref[...] = jnp.where(position >= end, end, start_ref[...])
        return end

    lax.fori_loop(0, episodes, add_episode, jnp.int32(0))

    def out_columns(k, g, piece):
        return pl.ds(pl.multiple_of(((k * 2 + g) * GROUP + piece * STACK) * HEAD, HEAD), wide)

    def staged(u, piece):
        return stage_ref.at[u, :, pl.ds(piece * wide, wide)]

    def out_copy(u, g, piece, to, source):
        return pltpu.make_async_remote_copy(
            src_ref=staged(u, piece), dst_ref=out_ref.at[:, out_columns(source, g, piece)],
            send_sem=out_send.at[u, piece], recv_sem=out_recv.at[g, source, piece],
            device_id=(seq, to), device_id_type=MESH,
        )

    def own_copy(u, g, piece):
        return pltpu.make_async_copy(
            staged(u, piece), out_ref.at[:, out_columns(kvh, g, piece)], own_sem.at[g, piece]
        )

    def target(step):
        late, odd = step // 2, step % 2
        upper, low = kvh // 2, kvh % 2
        far = (1 - upper) * (3 - odd) + upper * odd
        near = 2 * upper + (1 - low) * (1 - odd) + low * odd
        return (1 - late) * far + late * near

    def unit(g, step):
        r = target(step)
        u = 4 * g + step
        base = pl.multiple_of(r * rows, rows)
        begin = start_ref[pl.ds(base, rows), 0:1] - (seq * block - WINDOW + base)
        q = [q_ref[g, j, pl.ds(base, rows), :] for j in range(GROUP)]

        def finish(piece, outs):
            for j in range(STACK):
                at = (piece * STACK + j) * HEAD
                stage_ref[u, :, at:at + HEAD] = outs[j]

            @pl.when(step < 3)
            def _():
                out_copy(u, g, piece, r, kvh).start()

            @pl.when(step == 3)
            def _():
                own_copy(u, g, piece).start()

        attend(q, kv_refs[g], base, begin, scale, finish)

    @pl.when(first)
    def _():
        @pl.when(seq == half - 2)
        def _():
            pass_slot(0, 3, 1, 2, 0).wait_send()
            cross(1, half - 2, 0)
        pass_on(0)
        ahead_even(1)

    @pl.when(second)
    def _():
        relay(0)

        @pl.when(has_next)
        def _():
            pass_slot(0, 3, 2, 1, 0).wait_send()
        ahead_second(0)
        for source, sem in ((half - 1, 0), (half - 3, 1)):
            @pl.when(seq == source)
            def _():
                cross(1, source, sem)
        relay(1)

    window_in(0)

    @pl.when(second)
    def _():
        ahead_odd(1)

    @pl.loop(0, 4)
    def _(step):
        @pl.when(first & (step == 1))
        def _():
            pass_on(1)

        @pl.when(second & (step == 1))
        def _():
            ahead_second(1)

        unit(0, step)

    window_in(1)

    @pl.loop(0, 4)
    def _(step):
        unit(1, step)

    @pl.when(first)
    def _():
        @pl.when(has_next & (seq != half - 2))
        def _():
            pass_slot(0, 3, 1, 2, 0).wait_send()

        @pl.when(has_next)
        def _():
            pass_slot(1, 3, 1, 2, 0).wait_send()
        for g in range(2):
            @pl.when(seq == half)
            def _():
                pass_slot(g, 2, 0, 2, 4).wait_send()
            for sem in range(1, 4):
                pass_slot(g, 3, 2, 1, sem).wait_send()

    @pl.when(second)
    def _():
        @pl.when(has_next)
        def _():
            pass_slot(1, 3, 2, 1, 0).wait_send()
        for g in range(2):
            @pl.when(has_second & (seq != half - 1))
            def _():
                to_second(g).wait_send()
            for route in relays:
                @pl.when(seq == route[3])
                def _():
                    from_relay(g, route).wait_send()

    for g in range(2):
        for piece in range(pieces):
            for step in range(3):
                out_copy(4 * g + step, g, piece, kvh, kvh).wait_send()
            own_copy(4 * g + 3, g, piece).wait()
            for step in range(1, n_kvh):
                source = lax.rem(kvh + step, n_kvh)
                out_copy(0, g, piece, source, source).wait_recv()


def body(n_chips, n_kvh, queries, keys, values, episode_lengths):
    block = keys.shape[0]
    rows = block // n_kvh
    width = queries.shape[1]
    hbm = pl.BlockSpec(memory_space=pltpu.HBM)
    return pl.pallas_call(
        functools.partial(kernel, n_chips, n_kvh),
        out_shape=pltpu.VMEM((rows, width * n_kvh), jnp.bfloat16),
        in_specs=[hbm, hbm, hbm, hbm],
        out_specs=pl.BlockSpec(memory_space=pl.ANY),
        scratch_shapes=[
            pltpu.SMEM(episode_lengths.shape, jnp.int32),
            pltpu.VMEM((2, GROUP, block, HEAD), jnp.bfloat16),
            pltpu.VMEM((4 * block, 2 * HEAD), jnp.bfloat16),
            pltpu.VMEM((4 * block, 2 * HEAD), jnp.bfloat16),
            pltpu.VMEM((2, block // 2, 2 * HEAD), jnp.bfloat16),
            pltpu.VMEM((block, HEAD), jnp.int32),
            pltpu.VMEM((8, rows, GROUP * HEAD), jnp.bfloat16),
            pltpu.SemaphoreType.DMA((13,)),
            pltpu.SemaphoreType.DMA((2, 5)),
            pltpu.SemaphoreType.DMA((2, 3)),
            pltpu.SemaphoreType.DMA((2,)),
            pltpu.SemaphoreType.DMA((8, GROUP // STACK)),
            pltpu.SemaphoreType.DMA((2, n_kvh, GROUP // STACK)),
            pltpu.SemaphoreType.DMA((2, GROUP // STACK)),
        ],
        compiler_params=pltpu.CompilerParams(
            collective_id=0, has_side_effects=True, vmem_limit_bytes=40 << 20
        ),
        name="attention",
    )(*(
        pltpu.with_memory_space_constraint(x, pltpu.HBM)
        for x in (episode_lengths, queries, keys, values)
    ))


def solution(mesh):
    return jax.shard_map(
        functools.partial(body, mesh.shape["seq"] // 2, mesh.shape["kvh"]),
        mesh=mesh,
        in_specs=(P("seq", "kvh"), P("seq", "kvh"), P("seq", "kvh"), P()),
        out_specs=P(("seq", "kvh"), None),
        check_vma=False,
    )
```

```python
import functools
import math

import jax
import jax.numpy as jnp
from jax import lax
from jax.experimental import pallas as pl
from jax.experimental.pallas import tpu as pltpu
from jax.sharding import PartitionSpec as P

HEAD = 128
GROUP = 4
WINDOW = 1536
MESH = pl.DeviceIdType.MESH
MASKED = -1e30
STACK = 2


def attend(q, kv_ref, base, begin, scale, finish):
    stack = STACK
    rows = begin.shape[0]
    row = lax.broadcasted_iota(jnp.int32, (rows, rows), 0)
    col = lax.broadcasted_iota(jnp.int32, (rows, rows), 1)
    last = col <= row
    edge_seen = jnp.where(last, col + WINDOW, col) >= begin
    middle_seen = lax.broadcasted_iota(jnp.int32, (rows, WINDOW - rows), 1) + rows >= begin
    last, edge_seen, middle_seen = (
        jnp.concatenate([mask] * stack, 0) for mask in (last, edge_seen, middle_seen)
    )

    def part(offset, count):
        span = pl.ds(base + offset, count)
        return kv_ref[span, 0:HEAD], kv_ref[span, HEAD:2 * HEAD]

    first_k, first_v = part(0, rows)
    middle_k, middle_v = part(rows, WINDOW - rows)
    last_k, last_v = part(WINDOW, rows)

    def score(lhs, keys):
        return lax.dot_general(
            lhs, keys, (((1,), (1,)), ((), ())), preferred_element_type=jnp.float32
        )

    def add_up(weights, values):
        return jnp.dot(weights, values, preferred_element_type=jnp.float32)

    for j in range(0, GROUP, stack):
        lhs = jnp.concatenate(q[j:j + stack], 0)
        edge = jnp.where(last, score(lhs, last_k), score(lhs, first_k))
        edge = jnp.where(edge_seen, edge, MASKED)
        middle = jnp.where(middle_seen, score(lhs, middle_k), MASKED)
        top = jnp.maximum(
            jnp.max(middle, axis=1, keepdims=True), jnp.max(edge, axis=1, keepdims=True)
        )
        edge = jnp.exp2((edge - top) * scale)
        middle = jnp.exp2((middle - top) * scale)
        total = jnp.sum(middle, axis=1, keepdims=True) + jnp.sum(edge, axis=1, keepdims=True)
        edge = edge.astype(jnp.bfloat16)
        none = jnp.zeros_like(edge)
        summed = add_up(middle.astype(jnp.bfloat16), middle_v)
        summed += add_up(jnp.where(last, edge, none), last_v)
        summed += add_up(jnp.where(last, none, edge), first_v)
        out = (summed / total).astype(jnp.bfloat16)
        finish(j // stack, [out[i * rows:(i + 1) * rows] for i in range(stack)])


def crossing(n_seq):
    if n_seq != 128:
        return ()
    return (
        (63, 64, 2, 0, None), (63, 64, 2, 1, 119),
        (62, 64, 1, 0, 127), (62, 64, 1, 1, 79),
        (61, 64, 0, 0, None), (61, 64, 0, 1, 125),
        (63, 66, 0, 0, None), (63, 66, 0, 1, 111),
    )


def back(chip):
    return chip - 1 + 4 * ((3 - chip % 4) // 3)


def around(chip):
    return chip + 1 - 4 * ((chip % 4) // 3)


def targets(n_chips, n_kvh, routes):
    far = {route[1] // 2 for route in routes}
    sends = [set() for _ in range(2 * n_chips)]
    for chip in range(n_chips):
        sends[2 * chip].add(2 * chip + 1)
        if chip + 1 < n_chips and not any(r[0] == 2 * chip and r[2] == 1 for r in routes):
            sends[2 * chip].add(2 * chip + 2)
        if chip + 1 < n_chips and not any(r[0] == 2 * chip + 1 and r[2] == 2 for r in routes):
            sends[2 * chip + 1].add(2 * chip + 2)
        if chip + 2 < n_chips and chip + 2 not in far:
            by = 2 * back(chip) + 1
            sends[2 * chip + 1].add(by)
            sends[by].add(2 * chip + 4)
    for source, target, _, _, by in routes:
        if by is None:
            sends[source].add(target)
        else:
            sends[source].add(by)
            sends[by].add(target)
    return [len(s) + n_kvh - 1 for s in sends]


def one_of(seq, devices):
    found = seq == devices[0]
    for device in devices[1:]:
        found = found | (seq == device)
    return found


def kernel(
    n_chips, n_kvh, lengths_hbm, q_hbm, k_hbm, v_hbm, out_ref,
    lengths_ref, q_ref, kv0_ref, kv1_ref, relay_ref, second_ref, start_ref, stage_ref,
    load_sem, kv_send, kv_recv, relay_recv, second_recv, out_send, out_recv, own_sem,
):
    block = k_hbm.shape[0]
    rows = block // n_kvh
    wide = STACK * HEAD
    pieces = GROUP // STACK
    episodes = lengths_ref.shape[0]
    seq = lax.axis_index("seq")
    kvh = lax.axis_index("kvh")
    chip = seq // 2
    first = lax.rem(seq, 2) == 0
    second = lax.rem(seq, 2) == 1
    n_seq = 2 * n_chips
    part = block // 2
    routes = crossing(n_seq)
    relays = [route for route in routes if route[4] is not None]
    scale = math.log2(math.e) / math.sqrt(HEAD)
    kv_refs = (kv0_ref, kv1_ref)

    def slot(g, i):
        return kv_refs[g].at[pl.ds(i * block, block)]

    own = []
    for g in range(2):
        for i, src in enumerate((k_hbm, v_hbm)):
            own.append(pltpu.make_async_copy(
                src.at[:, pl.ds(g * HEAD, HEAD)],
                kv_refs[g].at[pl.ds(3 * block, block), pl.ds(i * HEAD, HEAD)],
                load_sem.at[2 * g + i],
            ))
    later = [pltpu.make_async_copy(lengths_hbm, lengths_ref, load_sem.at[4])]
    for g in range(2):
        for j in range(GROUP):
            later.append(pltpu.make_async_copy(
                q_hbm.at[:, pl.ds((g * GROUP + j) * HEAD, HEAD)],
                q_ref.at[g, j],
                load_sem.at[5 + g * GROUP + j],
            ))
    for copy in own + later:
        copy.start()

    barrier = pltpu.get_barrier_semaphore()

    def greet(s, k):
        pl.semaphore_signal(barrier, inc=1, device_id=(s, k), device_id_type=MESH)

    for step in range(1, n_kvh):
        greet(seq, lax.rem(kvh + step, n_kvh))

    def far(slot_there):
        devices = sorted({route[1] for route in routes if route[2] == slot_there})
        return one_of(seq, devices) if devices else seq < 0

    def leaves(slot_there):
        devices = sorted({route[0] for route in routes if route[2] == slot_there})
        return one_of(seq, devices) if devices else seq < 0

    no = jnp.logical_not
    has_next = chip < n_chips - 1
    has_second = (chip < n_chips - 2) & no(leaves(0))
    gets_second = first & (chip >= 2) & no(far(0))
    aim = around(chip) + 2
    passes = second & (aim < n_chips)
    for device in sorted({route[1] for route in routes if route[2] == 0}):
        passes = passes & (aim != device // 2)

    @pl.when(first & (chip >= 1) & no(far(2)))
    def _():
        greet(seq - 1, kvh)

    @pl.when(first & (chip >= 1) & no(far(1)))
    def _():
        greet(seq - 2, kvh)

    @pl.when(gets_second)
    def _():
        greet(2 * back(chip - 2) + 1, kvh)

    @pl.when(second)
    def _():
        greet(seq - 1, kvh)

    @pl.when(passes)
    def _():
        greet(2 * aim - 3, kvh)

    greeted = set()
    for source, target_seq, _, _, by in routes:
        for receiver, sender in ((target_seq, source if by is None else by), (by, source)):
            if receiver is not None and (receiver, sender) not in greeted:
                greeted.add((receiver, sender))

                @pl.when(seq == receiver)
                def _():
                    greet(sender, kvh)

    counts = targets(n_chips, n_kvh, routes)
    usual = (n_kvh + 1, n_kvh + 2)
    odd_ones = [s for s in range(n_seq) if counts[s] != usual[s % 2]]
    for count in sorted({counts[s] for s in odd_ones}):
        @pl.when(one_of(seq, [s for s in odd_ones if counts[s] == count]))
        def _():
            pl.semaphore_wait(barrier, count)

    for parity in range(2):
        @pl.when((first, second)[parity] & no(one_of(seq, odd_ones)))
        def _():
            pl.semaphore_wait(barrier, usual[parity])

    def send(g, src, dst, to, sem, recv):
        return pltpu.make_async_remote_copy(
            src_ref=src, dst_ref=dst, send_sem=kv_send.at[g, sem], recv_sem=recv,
            device_id=(to, kvh), device_id_type=MESH,
        )

    def pass_slot(g, here, there, by, sem):
        return send(g, slot(g, here), slot(g, there), seq + by, sem, kv_recv.at[g, there])

    def arrived(g, there):
        pass_slot(g, there, there, 1, 0).wait_recv()

    def to_sibling(g):
        return pass_slot(g, 3, 2, 1, 1)

    def to_second(g):
        return send(g, slot(g, 3), second_ref.at[g], 2 * back(chip) + 1, 1, second_recv.at[g])

    def from_second(g):
        return send(g, second_ref.at[g], slot(g, 0), 2 * aim, 3, kv_recv.at[g, 0])

    def rows_of(g, i, piece):
        return kv_refs[g].at[pl.ds(i * block + piece * part, part)]

    def to_relay(g, route, sem):
        return send(g, rows_of(g, 3, route[3]), relay_ref.at[g], route[4], sem, relay_recv.at[g])

    def from_relay(g, route):
        _, to, there, piece, _ = route
        return send(g, relay_ref.at[g], rows_of(g, there, piece), to, 2, kv_recv.at[g, there])

    def cross(g, there):
        for route in routes:
            source, to, into, piece, by = route
            if into != there:
                continue
            sem = 1 if there == 0 else 0

            @pl.when(seq == source)
            def _():
                if by is None:
                    send(
                        g, rows_of(g, 3, piece), rows_of(g, there, piece), to, sem,
                        kv_recv.at[g, there],
                    ).start()
                else:
                    to_relay(g, route, sem).start()

    def to_next(g):
        @pl.when(first & has_next & no(leaves(1)))
        def _():
            pass_slot(g, 3, 1, 2, 0).start()

        @pl.when(second & has_next & no(leaves(2)))
        def _():
            pass_slot(g, 3, 2, 1, 0).start()

        cross(g, 1)
        cross(g, 2)

        @pl.when(first)
        def _():
            to_sibling(g).start()

    def next_left(g):
        @pl.when(has_next)
        def _():
            pass_slot(g, 3, 1, 1, 0).wait_send()

    def ahead_second(g):
        @pl.when(second & has_second)
        def _():
            to_second(g).start()
        cross(g, 0)

    def second_left(g):
        @pl.when(second & (chip < n_chips - 2))
        def _():
            to_second(g).wait_send()

    def relay(g):
        for route in relays:
            @pl.when(seq == route[4])
            def _():
                to_relay(g, route, 0).wait_recv()
                from_relay(g, route).start()

    def relay_second(g):
        @pl.when(passes)
        def _():
            to_second(g).wait_recv()
            from_second(g).start()

    def pass_on(g):
        @pl.when(chip >= 1)
        def _():
            arrived(g, 2)
        pass_slot(g, 2, 1, 1, 2).start()

        @pl.when(chip >= 1)
        def _():
            arrived(g, 1)
        pass_slot(g, 1, 0, 1, 3).start()

    def window_in(g):
        @pl.when(first & (chip >= 2))
        def _():
            arrived(g, 0)

        @pl.when(second)
        def _():
            for i in range(3):
                arrived(g, i)

    for copy in own:
        copy.wait()

    to_next(0)
    ahead_second(0)

    @pl.when(first & (chip == 0))
    def _():
        for ref in kv_refs:
            ref[0:3 * block, :] = jnp.zeros((3 * block, 2 * HEAD), jnp.bfloat16)

    @pl.when(first & (chip == 1))
    def _():
        for ref in kv_refs:
            ref[0:block, :] = jnp.zeros((block, 2 * HEAD), jnp.bfloat16)

    for copy in later:
        copy.wait()
    position = seq * block + lax.broadcasted_iota(jnp.int32, (block, HEAD), 0)
    start_ref[...] = jnp.zeros((block, HEAD), jnp.int32)

    def add_episode(e, end):
        end = end + lengths_ref[e]
        start_ref[...] = jnp.where(position >= end, end, start_ref[...])
        return end

    lax.fori_loop(0, episodes, add_episode, jnp.int32(0))

    def out_columns(k, g, piece):
        return pl.ds(pl.multiple_of(((k * 2 + g) * GROUP + piece * STACK) * HEAD, HEAD), wide)

    def staged(u, piece):
        return stage_ref.at[u, :, pl.ds(piece * wide, wide)]

    def out_copy(u, g, piece, to, source):
        return pltpu.make_async_remote_copy(
            src_ref=staged(u, piece), dst_ref=out_ref.at[:, out_columns(source, g, piece)],
            send_sem=out_send.at[u, piece], recv_sem=out_recv.at[g, source, piece],
            device_id=(seq, to), device_id_type=MESH,
        )

    def own_copy(u, g, piece):
        return pltpu.make_async_copy(
            staged(u, piece), out_ref.at[:, out_columns(kvh, g, piece)], own_sem.at[g, piece]
        )

    def target(step):
        late, odd = step // 2, step % 2
        upper, low = kvh // 2, kvh % 2
        far = (1 - upper) * (3 - odd) + upper * odd
        near = 2 * upper + (1 - low) * (1 - odd) + low * odd
        return (1 - late) * far + late * near

    def unit(g, step):
        r = target(step)
        u = 4 * g + step
        base = pl.multiple_of(r * rows, rows)
        begin = start_ref[pl.ds(base, rows), 0:1] - (seq * block - WINDOW + base)
        q = [q_ref[g, j, pl.ds(base, rows), :] for j in range(GROUP)]

        def finish(piece, outs):
            for j in range(STACK):
                at = (piece * STACK + j) * HEAD
                stage_ref[u, :, at:at + HEAD] = outs[j]

            @pl.when(step < 3)
            def _():
                out_copy(u, g, piece, r, kvh).start()

            @pl.when(step == 3)
            def _():
                own_copy(u, g, piece).start()

        attend(q, kv_refs[g], base, begin, scale, finish)

    relay(0)
    relay_second(0)
    next_left(0)
    to_next(1)

    @pl.when(first)
    def _():
        pass_on(0)
    second_left(0)
    ahead_second(1)
    relay(1)
    window_in(0)

    @pl.loop(0, 4)
    def _(step):
        @pl.when(step == 1)
        def _():
            relay_second(1)

        @pl.when(first & (step == 2))
        def _():
            pass_on(1)

        unit(0, step)

    window_in(1)

    @pl.loop(0, 4)
    def _(step):
        unit(1, step)

    next_left(1)
    second_left(1)
    for g in range(2):
        @pl.when(first)
        def _():
            for sem in range(1, 4):
                pass_slot(g, 3, 2, 1, sem).wait_send()

        @pl.when(passes)
        def _():
            from_second(g).wait_send()
        for route in relays:
            @pl.when(seq == route[4])
            def _():
                from_relay(g, route).wait_send()

    for g in range(2):
        for piece in range(pieces):
            for step in range(3):
                out_copy(4 * g + step, g, piece, kvh, kvh).wait_send()
            own_copy(4 * g + 3, g, piece).wait()
            for step in range(1, n_kvh):
                source = lax.rem(kvh + step, n_kvh)
                out_copy(0, g, piece, source, source).wait_recv()


def body(n_chips, n_kvh, queries, keys, values, episode_lengths):
    block = keys.shape[0]
    rows = block // n_kvh
    width = queries.shape[1]
    hbm = pl.BlockSpec(memory_space=pltpu.HBM)
    return pl.pallas_call(
        functools.partial(kernel, n_chips, n_kvh),
        out_shape=pltpu.VMEM((rows, width * n_kvh), jnp.bfloat16),
        in_specs=[hbm, hbm, hbm, hbm],
        out_specs=pl.BlockSpec(memory_space=pl.ANY),
        scratch_shapes=[
            pltpu.SMEM(episode_lengths.shape, jnp.int32),
            pltpu.VMEM((2, GROUP, block, HEAD), jnp.bfloat16),
            pltpu.VMEM((4 * block, 2 * HEAD), jnp.bfloat16),
            pltpu.VMEM((4 * block, 2 * HEAD), jnp.bfloat16),
            pltpu.VMEM((2, block // 2, 2 * HEAD), jnp.bfloat16),
            pltpu.VMEM((2, block, 2 * HEAD), jnp.bfloat16),
            pltpu.VMEM((block, HEAD), jnp.int32),
            pltpu.VMEM((8, rows, GROUP * HEAD), jnp.bfloat16),
            pltpu.SemaphoreType.DMA((13,)),
            pltpu.SemaphoreType.DMA((2, 4)),
            pltpu.SemaphoreType.DMA((2, 3)),
            pltpu.SemaphoreType.DMA((2,)),
            pltpu.SemaphoreType.DMA((2,)),
            pltpu.SemaphoreType.DMA((8, GROUP // STACK)),
            pltpu.SemaphoreType.DMA((2, n_kvh, GROUP // STACK)),
            pltpu.SemaphoreType.DMA((2, GROUP // STACK)),
        ],
        compiler_params=pltpu.CompilerParams(
            collective_id=0, has_side_effects=True, vmem_limit_bytes=40 << 20
        ),
        name="attention",
    )(*(
        pltpu.with_memory_space_constraint(x, pltpu.HBM)
        for x in (episode_lengths, queries, keys, values)
    ))


def solution(mesh):
    return jax.shard_map(
        functools.partial(body, mesh.shape["seq"] // 2, mesh.shape["kvh"]),
        mesh=mesh,
        in_specs=(P("seq", "kvh"), P("seq", "kvh"), P("seq", "kvh"), P()),
        out_specs=P(("seq", "kvh"), None),
        check_vma=False,
    )
```

```python
import functools
import math

import jax
import jax.numpy as jnp
from jax import lax
from jax.experimental import pallas as pl
from jax.experimental.pallas import tpu as pltpu
from jax.sharding import PartitionSpec as P

HEAD = 128
GROUP = 4
WINDOW = 1536
MESH = pl.DeviceIdType.MESH
MASKED = -1e30
STACK = 2


def attend(q, kv_ref, base, begin, scale, finish):
    stack = STACK
    rows = begin.shape[0]
    row = lax.broadcasted_iota(jnp.int32, (rows, rows), 0)
    col = lax.broadcasted_iota(jnp.int32, (rows, rows), 1)
    last = col <= row
    edge_seen = jnp.where(last, col + WINDOW, col) >= begin
    middle_seen = lax.broadcasted_iota(jnp.int32, (rows, WINDOW - rows), 1) + rows >= begin
    last, edge_seen, middle_seen = (
        jnp.concatenate([mask] * stack, 0) for mask in (last, edge_seen, middle_seen)
    )

    def part(offset, count):
        span = pl.ds(base + offset, count)
        return kv_ref[span, 0:HEAD], kv_ref[span, HEAD:2 * HEAD]

    first_k, first_v = part(0, rows)
    middle_k, middle_v = part(rows, WINDOW - rows)
    last_k, last_v = part(WINDOW, rows)

    def score(lhs, keys):
        return lax.dot_general(
            lhs, keys, (((1,), (1,)), ((), ())), preferred_element_type=jnp.float32
        )

    def add_up(weights, values):
        return jnp.dot(weights, values, preferred_element_type=jnp.float32)

    for j in range(0, GROUP, stack):
        lhs = jnp.concatenate(q[j:j + stack], 0)
        edge = jnp.where(last, score(lhs, last_k), score(lhs, first_k))
        edge = jnp.where(edge_seen, edge, MASKED)
        middle = jnp.where(middle_seen, score(lhs, middle_k), MASKED)
        top = jnp.maximum(
            jnp.max(middle, axis=1, keepdims=True), jnp.max(edge, axis=1, keepdims=True)
        )
        edge = jnp.exp2((edge - top) * scale)
        middle = jnp.exp2((middle - top) * scale)
        total = jnp.sum(middle, axis=1, keepdims=True) + jnp.sum(edge, axis=1, keepdims=True)
        edge = edge.astype(jnp.bfloat16)
        none = jnp.zeros_like(edge)
        summed = add_up(middle.astype(jnp.bfloat16), middle_v)
        summed += add_up(jnp.where(last, edge, none), last_v)
        summed += add_up(jnp.where(last, none, edge), first_v)
        out = (summed / total).astype(jnp.bfloat16)
        finish(j // stack, [out[i * rows:(i + 1) * rows] for i in range(stack)])


def crossing(n_seq):
    if n_seq != 128:
        return ()
    return (
        (63, 64, 2, 0, None), (63, 64, 2, 1, 119),
        (62, 64, 1, 0, 127), (62, 64, 1, 1, 103),
        (61, 64, 0, 0, None), (61, 64, 0, 1, 125),
        (63, 66, 0, 0, 79), (63, 66, 0, 1, 111),
    )


def back(chip):
    return chip - 1 + 4 * ((3 - chip % 4) // 3)


def around(chip):
    return chip + 1 - 4 * ((chip % 4) // 3)


def targets(n_chips, n_kvh, routes):
    far = {route[1] // 2 for route in routes}
    sends = [set() for _ in range(2 * n_chips)]
    for chip in range(n_chips):
        sends[2 * chip].add(2 * chip + 1)
        if chip + 1 < n_chips and not any(r[0] == 2 * chip and r[2] == 1 for r in routes):
            sends[2 * chip].add(2 * chip + 2)
        if chip + 1 < n_chips and not any(r[0] == 2 * chip + 1 and r[2] == 2 for r in routes):
            sends[2 * chip + 1].add(2 * chip + 2)
        if chip + 2 < n_chips and chip + 2 not in far:
            by = 2 * back(chip) + 1
            sends[2 * chip + 1].add(by)
            sends[by].add(2 * chip + 4)
    for source, target, _, _, by in routes:
        if by is None:
            sends[source].add(target)
        else:
            sends[source].add(by)
            sends[by].add(target)
    return [len(s) + n_kvh - 1 for s in sends]


def one_of(seq, devices):
    found = seq == devices[0]
    for device in devices[1:]:
        found = found | (seq == device)
    return found


def kernel(
    n_chips, n_kvh, lengths_hbm, q_hbm, k_hbm, v_hbm, out_ref,
    lengths_ref, q_ref, kv0_ref, kv1_ref, relay_ref, second_ref, start_ref, stage_ref,
    load_sem, kv_send, kv_recv, relay_recv, second_recv, out_send, out_recv, own_sem,
):
    block = k_hbm.shape[0]
    rows = block // n_kvh
    wide = STACK * HEAD
    pieces = GROUP // STACK
    episodes = lengths_ref.shape[0]
    seq = lax.axis_index("seq")
    kvh = lax.axis_index("kvh")
    chip = seq // 2
    first = lax.rem(seq, 2) == 0
    second = lax.rem(seq, 2) == 1
    n_seq = 2 * n_chips
    part = block // 2
    routes = crossing(n_seq)
    relays = [route for route in routes if route[4] is not None]
    scale = math.log2(math.e) / math.sqrt(HEAD)
    kv_refs = (kv0_ref, kv1_ref)

    def slot(g, i):
        return kv_refs[g].at[pl.ds(i * block, block)]

    own = []
    for g in range(2):
        for i, src in enumerate((k_hbm, v_hbm)):
            own.append(pltpu.make_async_copy(
                src.at[:, pl.ds(g * HEAD, HEAD)],
                kv_refs[g].at[pl.ds(3 * block, block), pl.ds(i * HEAD, HEAD)],
                load_sem.at[2 * g + i],
            ))
    later = [pltpu.make_async_copy(lengths_hbm, lengths_ref, load_sem.at[4])]
    for g in range(2):
        for j in range(GROUP):
            later.append(pltpu.make_async_copy(
                q_hbm.at[:, pl.ds((g * GROUP + j) * HEAD, HEAD)],
                q_ref.at[g, j],
                load_sem.at[5 + g * GROUP + j],
            ))
    for copy in own + later:
        copy.start()

    barrier = pltpu.get_barrier_semaphore()

    def greet(s, k):
        pl.semaphore_signal(barrier, inc=1, device_id=(s, k), device_id_type=MESH)

    for step in range(1, n_kvh):
        greet(seq, lax.rem(kvh + step, n_kvh))

    def far(slot_there):
        devices = sorted({route[1] for route in routes if route[2] == slot_there})
        return one_of(seq, devices) if devices else seq < 0

    def leaves(slot_there):
        devices = sorted({route[0] for route in routes if route[2] == slot_there})
        return one_of(seq, devices) if devices else seq < 0

    no = jnp.logical_not
    has_next = chip < n_chips - 1
    has_second = (chip < n_chips - 2) & no(leaves(0))
    gets_second = first & (chip >= 2) & no(far(0))
    aim = around(chip) + 2
    passes = second & (aim < n_chips)
    for device in sorted({route[1] for route in routes if route[2] == 0}):
        passes = passes & (aim != device // 2)

    @pl.when(first & (chip >= 1) & no(far(2)))
    def _():
        greet(seq - 1, kvh)

    @pl.when(first & (chip >= 1) & no(far(1)))
    def _():
        greet(seq - 2, kvh)

    @pl.when(gets_second)
    def _():
        greet(2 * back(chip - 2) + 1, kvh)

    @pl.when(second)
    def _():
        greet(seq - 1, kvh)

    @pl.when(passes)
    def _():
        greet(2 * aim - 3, kvh)

    greeted = set()
    for source, target_seq, _, _, by in routes:
        for receiver, sender in ((target_seq, source if by is None else by), (by, source)):
            if receiver is not None and (receiver, sender) not in greeted:
                greeted.add((receiver, sender))

                @pl.when(seq == receiver)
                def _():
                    greet(sender, kvh)

    counts = targets(n_chips, n_kvh, routes)
    usual = (n_kvh + 1, n_kvh + 2)
    odd_ones = [s for s in range(n_seq) if counts[s] != usual[s % 2]]
    for count in sorted({counts[s] for s in odd_ones}):
        @pl.when(one_of(seq, [s for s in odd_ones if counts[s] == count]))
        def _():
            pl.semaphore_wait(barrier, count)

    for parity in range(2):
        @pl.when((first, second)[parity] & no(one_of(seq, odd_ones)))
        def _():
            pl.semaphore_wait(barrier, usual[parity])

    def send(g, src, dst, to, sem, recv):
        return pltpu.make_async_remote_copy(
            src_ref=src, dst_ref=dst, send_sem=kv_send.at[g, sem], recv_sem=recv,
            device_id=(to, kvh), device_id_type=MESH,
        )

    def pass_slot(g, here, there, by, sem):
        return send(g, slot(g, here), slot(g, there), seq + by, sem, kv_recv.at[g, there])

    def arrived(g, there):
        pass_slot(g, there, there, 1, 0).wait_recv()

    def to_sibling(g):
        return pass_slot(g, 3, 2, 1, 1)

    def to_second(g):
        return send(g, slot(g, 3), second_ref.at[g], 2 * back(chip) + 1, 1, second_recv.at[g])

    def from_second(g):
        return send(g, second_ref.at[g], slot(g, 0), 2 * aim, 3, kv_recv.at[g, 0])

    def rows_of(g, i, piece):
        return kv_refs[g].at[pl.ds(i * block + piece * part, part)]

    def to_relay(g, route, sem):
        return send(g, rows_of(g, 3, route[3]), relay_ref.at[g], route[4], sem, relay_recv.at[g])

    def from_relay(g, route):
        _, to, there, piece, _ = route
        return send(g, relay_ref.at[g], rows_of(g, there, piece), to, 2, kv_recv.at[g, there])

    def cross(g, there):
        for route in routes:
            source, to, into, piece, by = route
            if into != there:
                continue
            sem = 1 if there == 0 else 0

            @pl.when(seq == source)
            def _():
                if by is None:
                    send(
                        g, rows_of(g, 3, piece), rows_of(g, there, piece), to, sem,
                        kv_recv.at[g, there],
                    ).start()
                else:
                    to_relay(g, route, sem).start()

    def to_next(g):
        @pl.when(first & has_next & no(leaves(1)))
        def _():
            pass_slot(g, 3, 1, 2, 0).start()

        @pl.when(second & has_next & no(leaves(2)))
        def _():
            pass_slot(g, 3, 2, 1, 0).start()

        cross(g, 1)
        cross(g, 2)

        @pl.when(first)
        def _():
            to_sibling(g).start()

    def next_left(g):
        @pl.when(has_next)
        def _():
            pass_slot(g, 3, 1, 1, 0).wait_send()

    def ahead_second(g):
        @pl.when(second & has_second)
        def _():
            to_second(g).start()
        cross(g, 0)

    def second_left(g):
        @pl.when(second & (chip < n_chips - 2))
        def _():
            to_second(g).wait_send()

    def relay(g):
        for route in relays:
            @pl.when(seq == route[4])
            def _():
                to_relay(g, route, 0).wait_recv()
                from_relay(g, route).start()

    def relay_second(g):
        @pl.when(passes)
        def _():
            to_second(g).wait_recv()
            from_second(g).start()

    def pass_on(g):
        @pl.when(chip >= 1)
        def _():
            arrived(g, 2)
        pass_slot(g, 2, 1, 1, 2).start()

        @pl.when(chip >= 1)
        def _():
            arrived(g, 1)
        pass_slot(g, 1, 0, 1, 3).start()

    def window_in(g):
        @pl.when(first & (chip >= 2))
        def _():
            arrived(g, 0)

        @pl.when(second)
        def _():
            for i in range(3):
                arrived(g, i)

    for copy in own:
        copy.wait()

    to_next(0)
    ahead_second(0)

    @pl.when(first & (chip == 0))
    def _():
        for ref in kv_refs:
            ref[0:3 * block, :] = jnp.zeros((3 * block, 2 * HEAD), jnp.bfloat16)

    @pl.when(first & (chip == 1))
    def _():
        for ref in kv_refs:
            ref[0:block, :] = jnp.zeros((block, 2 * HEAD), jnp.bfloat16)

    for copy in later:
        copy.wait()
    position = seq * block + lax.broadcasted_iota(jnp.int32, (block, HEAD), 0)
    start_ref[...] = jnp.zeros((block, HEAD), jnp.int32)

    def add_episode(e, end):
        end = end + lengths_ref[e]
        start_ref[...] = jnp.where(position >= end, end, start_ref[...])
        return end

    lax.fori_loop(0, episodes, add_episode, jnp.int32(0))

    def out_columns(k, g, piece):
        return pl.ds(pl.multiple_of(((k * 2 + g) * GROUP + piece * STACK) * HEAD, HEAD), wide)

    def staged(u, piece):
        return stage_ref.at[u, :, pl.ds(piece * wide, wide)]

    def out_copy(u, g, piece, to, source):
        return pltpu.make_async_remote_copy(
            src_ref=staged(u, piece), dst_ref=out_ref.at[:, out_columns(source, g, piece)],
            send_sem=out_send.at[u, piece], recv_sem=out_recv.at[g, source, piece],
            device_id=(seq, to), device_id_type=MESH,
        )

    def own_copy(u, g, piece):
        return pltpu.make_async_copy(
            staged(u, piece), out_ref.at[:, out_columns(kvh, g, piece)], own_sem.at[g, piece]
        )

    def target(step):
        late, odd = step // 2, step % 2
        upper, low = kvh // 2, kvh % 2
        far = (1 - upper) * (3 - odd) + upper * odd
        near = 2 * upper + (1 - low) * (1 - odd) + low * odd
        return (1 - late) * far + late * near

    def unit(g, step):
        r = target(step)
        u = 4 * g + step
        base = pl.multiple_of(r * rows, rows)
        begin = start_ref[pl.ds(base, rows), 0:1] - (seq * block - WINDOW + base)
        q = [q_ref[g, j, pl.ds(base, rows), :] for j in range(GROUP)]

        def finish(piece, outs):
            for j in range(STACK):
                at = (piece * STACK + j) * HEAD
                stage_ref[u, :, at:at + HEAD] = outs[j]

            @pl.when(step < 3)
            def _():
                out_copy(u, g, piece, r, kvh).start()

            @pl.when(step == 3)
            def _():
                own_copy(u, g, piece).start()

        attend(q, kv_refs[g], base, begin, scale, finish)

    sources = sorted({route[0] for route in routes})
    early = one_of(seq, sources) if sources else seq < 0

    @pl.when(early)
    def _():
        next_left(0)
        to_next(1)
        second_left(0)
        ahead_second(1)
    relay(0)
    relay_second(0)

    @pl.when(no(early))
    def _():
        next_left(0)
        to_next(1)

    @pl.when(first)
    def _():
        pass_on(0)

    @pl.when(no(early))
    def _():
        second_left(0)
        ahead_second(1)
    window_in(0)

    @pl.loop(0, 4)
    def _(step):
        @pl.when(step == 1)
        def _():
            relay(1)
            relay_second(1)

        @pl.when(first & (step == 2))
        def _():
            pass_on(1)

        unit(0, step)

    window_in(1)

    @pl.loop(0, 4)
    def _(step):
        unit(1, step)

    next_left(1)
    second_left(1)
    for g in range(2):
        @pl.when(first)
        def _():
            for sem in range(1, 4):
                pass_slot(g, 3, 2, 1, sem).wait_send()

        @pl.when(passes)
        def _():
            from_second(g).wait_send()
        for route in relays:
            @pl.when(seq == route[4])
            def _():
                from_relay(g, route).wait_send()

    for g in range(2):
        for piece in range(pieces):
            for step in range(3):
                out_copy(4 * g + step, g, piece, kvh, kvh).wait_send()
            own_copy(4 * g + 3, g, piece).wait()
            for step in range(1, n_kvh):
                source = lax.rem(kvh + step, n_kvh)
                out_copy(0, g, piece, source, source).wait_recv()


def body(n_chips, n_kvh, queries, keys, values, episode_lengths):
    block = keys.shape[0]
    rows = block // n_kvh
    width = queries.shape[1]
    hbm = pl.BlockSpec(memory_space=pltpu.HBM)
    return pl.pallas_call(
        functools.partial(kernel, n_chips, n_kvh),
        out_shape=pltpu.VMEM((rows, width * n_kvh), jnp.bfloat16),
        in_specs=[hbm, hbm, hbm, hbm],
        out_specs=pl.BlockSpec(memory_space=pl.ANY),
        scratch_shapes=[
            pltpu.SMEM(episode_lengths.shape, jnp.int32),
            pltpu.VMEM((2, GROUP, block, HEAD), jnp.bfloat16),
            pltpu.VMEM((4 * block, 2 * HEAD), jnp.bfloat16),
            pltpu.VMEM((4 * block, 2 * HEAD), jnp.bfloat16),
            pltpu.VMEM((2, block // 2, 2 * HEAD), jnp.bfloat16),
            pltpu.VMEM((2, block, 2 * HEAD), jnp.bfloat16),
            pltpu.VMEM((block, HEAD), jnp.int32),
            pltpu.VMEM((8, rows, GROUP * HEAD), jnp.bfloat16),
            pltpu.SemaphoreType.DMA((13,)),
            pltpu.SemaphoreType.DMA((2, 4)),
            pltpu.SemaphoreType.DMA((2, 3)),
            pltpu.SemaphoreType.DMA((2,)),
            pltpu.SemaphoreType.DMA((2,)),
            pltpu.SemaphoreType.DMA((8, GROUP // STACK)),
            pltpu.SemaphoreType.DMA((2, n_kvh, GROUP // STACK)),
            pltpu.SemaphoreType.DMA((2, GROUP // STACK)),
        ],
        compiler_params=pltpu.CompilerParams(
            collective_id=0, has_side_effects=True, vmem_limit_bytes=40 << 20
        ),
        name="attention",
    )(*(
        pltpu.with_memory_space_constraint(x, pltpu.HBM)
        for x in (episode_lengths, queries, keys, values)
    ))


def solution(mesh):
    return jax.shard_map(
        functools.partial(body, mesh.shape["seq"] // 2, mesh.shape["kvh"]),
        mesh=mesh,
        in_specs=(P("seq", "kvh"), P("seq", "kvh"), P("seq", "kvh"), P()),
        out_specs=P(("seq", "kvh"), None),
        check_vma=False,
    )
```

```python
import functools
import math

import jax
import jax.numpy as jnp
from jax import lax
from jax.experimental import pallas as pl
from jax.experimental.pallas import tpu as pltpu
from jax.sharding import PartitionSpec as P

HEAD = 128
GROUP = 4
WINDOW = 1536
MESH = pl.DeviceIdType.MESH
MASKED = -1e30
STACK = 2


def attend(q, kv_ref, base, begin, scale, finish):
    stack = STACK
    rows = begin.shape[0]
    row = lax.broadcasted_iota(jnp.int32, (rows, rows), 0)
    col = lax.broadcasted_iota(jnp.int32, (rows, rows), 1)
    last = col <= row
    edge_seen = jnp.where(last, col + WINDOW, col) >= begin
    middle_seen = lax.broadcasted_iota(jnp.int32, (rows, WINDOW - rows), 1) + rows >= begin
    last, edge_seen, middle_seen = (
        jnp.concatenate([mask] * stack, 0) for mask in (last, edge_seen, middle_seen)
    )

    def part(offset, count):
        span = pl.ds(base + offset, count)
        return kv_ref[span, 0:HEAD], kv_ref[span, HEAD:2 * HEAD]

    first_k, first_v = part(0, rows)
    middle_k, middle_v = part(rows, WINDOW - rows)
    last_k, last_v = part(WINDOW, rows)

    def score(lhs, keys):
        return lax.dot_general(
            lhs, keys, (((1,), (1,)), ((), ())), preferred_element_type=jnp.float32
        )

    def add_up(weights, values):
        return jnp.dot(weights, values, preferred_element_type=jnp.float32)

    for j in range(0, GROUP, stack):
        lhs = jnp.concatenate(q[j:j + stack], 0)
        edge = jnp.where(last, score(lhs, last_k), score(lhs, first_k))
        edge = jnp.where(edge_seen, edge, MASKED)
        middle = jnp.where(middle_seen, score(lhs, middle_k), MASKED)
        top = jnp.maximum(
            jnp.max(middle, axis=1, keepdims=True), jnp.max(edge, axis=1, keepdims=True)
        )
        edge = jnp.exp2((edge - top) * scale)
        middle = jnp.exp2((middle - top) * scale)
        total = jnp.sum(middle, axis=1, keepdims=True) + jnp.sum(edge, axis=1, keepdims=True)
        edge = edge.astype(jnp.bfloat16)
        none = jnp.zeros_like(edge)
        summed = add_up(middle.astype(jnp.bfloat16), middle_v)
        summed += add_up(jnp.where(last, edge, none), last_v)
        summed += add_up(jnp.where(last, none, edge), first_v)
        out = (summed / total).astype(jnp.bfloat16)
        finish(j // stack, [out[i * rows:(i + 1) * rows] for i in range(stack)])


def crossing(n_seq):
    if n_seq != 128:
        return ()
    return (
        (63, ((64, 2), (66, 0)), 0, 127), (63, ((64, 2), (66, 0)), 1, 119),
        (62, ((64, 1),), 0, None), (62, ((64, 1),), 1, 111),
        (61, ((64, 0),), 0, None), (61, ((64, 0),), 1, 125),
    )


def back(chip):
    return chip - 1 + 4 * ((3 - chip % 4) // 3)


def around(chip):
    return chip + 1 - 4 * ((chip % 4) // 3)


def targets(n_chips, n_kvh, routes):
    far = {to // 2 for route in routes for to, there in route[1] if there == 0}
    leaves = {(route[0], there) for route in routes for _, there in route[1]}
    sends = [set() for _ in range(2 * n_chips)]
    for chip in range(n_chips):
        sends[2 * chip].add(2 * chip + 1)
        if chip + 1 < n_chips and (2 * chip, 1) not in leaves:
            sends[2 * chip].add(2 * chip + 2)
        if chip + 1 < n_chips and (2 * chip + 1, 2) not in leaves:
            sends[2 * chip + 1].add(2 * chip + 2)
        if chip + 2 < n_chips and chip + 2 not in far:
            by = 2 * back(chip) + 1
            sends[2 * chip + 1].add(by)
            sends[by].add(2 * chip + 4)
    for source, to, _, by in routes:
        reached = {device for device, _ in to}
        if by is None:
            sends[source] |= reached
        else:
            sends[source].add(by)
            sends[by] |= reached
    return [len(s) + n_kvh - 1 for s in sends]


def one_of(seq, devices):
    found = seq == devices[0]
    for device in devices[1:]:
        found = found | (seq == device)
    return found


def kernel(
    n_chips, n_kvh, lengths_hbm, q_hbm, k_hbm, v_hbm, out_ref,
    lengths_ref, q_ref, kv0_ref, kv1_ref, relay_ref, second_ref, start_ref, stage_ref,
    load_sem, kv_send, kv_recv, relay_recv, second_recv, out_send, out_recv, own_sem,
):
    block = k_hbm.shape[0]
    rows = block // n_kvh
    wide = STACK * HEAD
    pieces = GROUP // STACK
    episodes = lengths_ref.shape[0]
    seq = lax.axis_index("seq")
    kvh = lax.axis_index("kvh")
    chip = seq // 2
    first = lax.rem(seq, 2) == 0
    second = lax.rem(seq, 2) == 1
    n_seq = 2 * n_chips
    part = block // 2
    routes = crossing(n_seq)
    relays = [route for route in routes if route[3] is not None]
    scale = math.log2(math.e) / math.sqrt(HEAD)
    kv_refs = (kv0_ref, kv1_ref)

    def slot(g, i):
        return kv_refs[g].at[pl.ds(i * block, block)]

    own = []
    for g in range(2):
        for i, src in enumerate((k_hbm, v_hbm)):
            own.append(pltpu.make_async_copy(
                src.at[:, pl.ds(g * HEAD, HEAD)],
                kv_refs[g].at[pl.ds(3 * block, block), pl.ds(i * HEAD, HEAD)],
                load_sem.at[2 * g + i],
            ))
    later = [pltpu.make_async_copy(lengths_hbm, lengths_ref, load_sem.at[4])]
    for g in range(2):
        for j in range(GROUP):
            later.append(pltpu.make_async_copy(
                q_hbm.at[:, pl.ds((g * GROUP + j) * HEAD, HEAD)],
                q_ref.at[g, j],
                load_sem.at[5 + g * GROUP + j],
            ))
    for copy in own + later:
        copy.start()

    barrier = pltpu.get_barrier_semaphore()

    def greet(s, k):
        pl.semaphore_signal(barrier, inc=1, device_id=(s, k), device_id_type=MESH)

    for step in range(1, n_kvh):
        greet(seq, lax.rem(kvh + step, n_kvh))

    def far(slot_there):
        devices = sorted({to for route in routes for to, there in route[1] if there == slot_there})
        return one_of(seq, devices) if devices else seq < 0

    def leaves(slot_there):
        devices = sorted({r[0] for r in routes for _, there in r[1] if there == slot_there})
        return one_of(seq, devices) if devices else seq < 0

    no = jnp.logical_not
    has_next = chip < n_chips - 1
    has_second = (chip < n_chips - 2) & no(leaves(0))
    sends_second = has_second
    for source in sorted({route[0] for route in routes if route[1][0][1] == 0}):
        sends_second = sends_second | (seq == source)
    gets_second = first & (chip >= 2) & no(far(0))
    aim = around(chip) + 2
    passes = second & (aim < n_chips)
    for device in sorted({to for route in routes for to, there in route[1] if there == 0}):
        passes = passes & (aim != device // 2)

    @pl.when(first & (chip >= 1) & no(far(2)))
    def _():
        greet(seq - 1, kvh)

    @pl.when(first & (chip >= 1) & no(far(1)))
    def _():
        greet(seq - 2, kvh)

    @pl.when(gets_second)
    def _():
        greet(2 * back(chip - 2) + 1, kvh)

    @pl.when(second)
    def _():
        greet(seq - 1, kvh)

    @pl.when(passes)
    def _():
        greet(2 * aim - 3, kvh)

    greeted = set()
    for source, to, _, by in routes:
        pairs = [(device, source if by is None else by) for device, _ in to]
        for receiver, sender in pairs + [(by, source)]:
            if receiver is not None and (receiver, sender) not in greeted:
                greeted.add((receiver, sender))

                @pl.when(seq == receiver)
                def _():
                    greet(sender, kvh)

    counts = targets(n_chips, n_kvh, routes)
    usual = (n_kvh + 1, n_kvh + 2)
    odd_ones = [s for s in range(n_seq) if counts[s] != usual[s % 2]]
    for count in sorted({counts[s] for s in odd_ones}):
        @pl.when(one_of(seq, [s for s in odd_ones if counts[s] == count]))
        def _():
            pl.semaphore_wait(barrier, count)

    for parity in range(2):
        @pl.when((first, second)[parity] & no(one_of(seq, odd_ones)))
        def _():
            pl.semaphore_wait(barrier, usual[parity])

    def send(g, src, dst, to, sem, recv):
        return pltpu.make_async_remote_copy(
            src_ref=src, dst_ref=dst, send_sem=kv_send.at[g, sem], recv_sem=recv,
            device_id=(to, kvh), device_id_type=MESH,
        )

    def pass_slot(g, here, there, by, sem):
        return send(g, slot(g, here), slot(g, there), seq + by, sem, kv_recv.at[g, there])

    def arrived(g, there):
        pass_slot(g, there, there, 1, 0).wait_recv()

    def to_sibling(g):
        return pass_slot(g, 3, 2, 1, 1)

    def to_second(g):
        return send(g, slot(g, 3), second_ref.at[g], 2 * back(chip) + 1, 1, second_recv.at[g])

    def from_second(g):
        return send(g, second_ref.at[g], slot(g, 0), 2 * aim, 3, kv_recv.at[g, 0])

    def rows_of(g, i, piece):
        return kv_refs[g].at[pl.ds(i * block + piece * part, part)]

    def to_relay(g, route, sem):
        return send(g, rows_of(g, 3, route[2]), relay_ref.at[g], route[3], sem, relay_recv.at[g])

    def from_relay(g, route):
        return [
            send(g, relay_ref.at[g], rows_of(g, there, route[2]), to, sem, kv_recv.at[g, there])
            for (to, there), sem in zip(route[1], (2, 4))
        ]

    def cross(g, slots, sem):
        for route in routes:
            source, ((to, there), *_), piece, by = route
            if there not in slots:
                continue

            @pl.when(seq == source)
            def _():
                if by is None:
                    send(
                        g, rows_of(g, 3, piece), rows_of(g, there, piece), to, sem,
                        kv_recv.at[g, there],
                    ).start()
                else:
                    to_relay(g, route, sem).start()

    def to_next(g):
        @pl.when(first & has_next & no(leaves(1)))
        def _():
            pass_slot(g, 3, 1, 2, 0).start()

        @pl.when(second & has_next & no(leaves(2)))
        def _():
            pass_slot(g, 3, 2, 1, 0).start()

        cross(g, (1, 2), 0)

        @pl.when(first)
        def _():
            to_sibling(g).start()

    def next_left(g):
        @pl.when(has_next)
        def _():
            pass_slot(g, 3, 1, 1, 0).wait_send()

    def ahead_second(g):
        @pl.when(second & has_second)
        def _():
            to_second(g).start()
        cross(g, (0,), 1)

    def second_left(g):
        @pl.when(second & sends_second)
        def _():
            to_second(g).wait_send()

    def relay(g):
        for route in relays:
            @pl.when(seq == route[3])
            def _():
                to_relay(g, route, 0).wait_recv()
                for copy in from_relay(g, route):
                    copy.start()

    def relay_second(g):
        @pl.when(passes)
        def _():
            to_second(g).wait_recv()
            from_second(g).start()

    def pass_on(g):
        @pl.when(chip >= 1)
        def _():
            arrived(g, 2)
        pass_slot(g, 2, 1, 1, 2).start()

        @pl.when(chip >= 1)
        def _():
            arrived(g, 1)
        pass_slot(g, 1, 0, 1, 3).start()

    def window_in(g):
        @pl.when(first & (chip >= 2))
        def _():
            arrived(g, 0)

        @pl.when(second)
        def _():
            for i in range(3):
                arrived(g, i)

    for copy in own:
        copy.wait()

    to_next(0)
    ahead_second(0)

    @pl.when(first & (chip == 0))
    def _():
        for ref in kv_refs:
            ref[0:3 * block, :] = jnp.zeros((3 * block, 2 * HEAD), jnp.bfloat16)

    @pl.when(first & (chip == 1))
    def _():
        for ref in kv_refs:
            ref[0:block, :] = jnp.zeros((block, 2 * HEAD), jnp.bfloat16)

    for copy in later:
        copy.wait()
    position = seq * block + lax.broadcasted_iota(jnp.int32, (block, HEAD), 0)
    start_ref[...] = jnp.zeros((block, HEAD), jnp.int32)

    def add_episode(e, end):
        end = end + lengths_ref[e]
        start_ref[...] = jnp.where(position >= end, end, start_ref[...])
        return end

    lax.fori_loop(0, episodes, add_episode, jnp.int32(0))

    def out_columns(k, g, piece):
        return pl.ds(pl.multiple_of(((k * 2 + g) * GROUP + piece * STACK) * HEAD, HEAD), wide)

    def staged(u, piece):
        return stage_ref.at[u, :, pl.ds(piece * wide, wide)]

    def out_copy(u, g, piece, to, source):
        return pltpu.make_async_remote_copy(
            src_ref=staged(u, piece), dst_ref=out_ref.at[:, out_columns(source, g, piece)],
            send_sem=out_send.at[u, piece], recv_sem=out_recv.at[g, source, piece],
            device_id=(seq, to), device_id_type=MESH,
        )

    def own_copy(u, g, piece):
        return pltpu.make_async_copy(
            staged(u, piece), out_ref.at[:, out_columns(kvh, g, piece)], own_sem.at[g, piece]
        )

    def target(step):
        late, odd = step // 2, step % 2
        upper, low = kvh // 2, kvh % 2
        far = (1 - upper) * (3 - odd) + upper * odd
        near = 2 * upper + (1 - low) * (1 - odd) + low * odd
        return (1 - late) * far + late * near

    def unit(g, step):
        r = target(step)
        u = 4 * g + step
        base = pl.multiple_of(r * rows, rows)
        begin = start_ref[pl.ds(base, rows), 0:1] - (seq * block - WINDOW + base)
        q = [q_ref[g, j, pl.ds(base, rows), :] for j in range(GROUP)]

        def finish(piece, outs):
            for j in range(STACK):
                at = (piece * STACK + j) * HEAD
                stage_ref[u, :, at:at + HEAD] = outs[j]

            @pl.when(step < 3)
            def _():
                out_copy(u, g, piece, r, kvh).start()

            @pl.when(step == 3)
            def _():
                own_copy(u, g, piece).start()

        attend(q, kv_refs[g], base, begin, scale, finish)

    sources = sorted({route[0] for route in routes})
    early = one_of(seq, sources) if sources else seq < 0

    @pl.when(early)
    def _():
        next_left(0)
        to_next(1)
        second_left(0)
        ahead_second(1)
    relay(0)
    relay_second(0)

    @pl.when(no(early))
    def _():
        next_left(0)
        to_next(1)

    @pl.when(first)
    def _():
        pass_on(0)

    @pl.when(no(early))
    def _():
        second_left(0)
        ahead_second(1)
    window_in(0)

    @pl.loop(0, 4)
    def _(step):
        @pl.when(step == 1)
        def _():
            relay(1)
            relay_second(1)

        @pl.when(first & (step == 2))
        def _():
            pass_on(1)

        unit(0, step)

    window_in(1)

    @pl.loop(0, 4)
    def _(step):
        unit(1, step)

    next_left(1)
    second_left(1)
    for g in range(2):
        @pl.when(first)
        def _():
            for sem in range(1, 4):
                pass_slot(g, 3, 2, 1, sem).wait_send()

        @pl.when(passes)
        def _():
            from_second(g).wait_send()
        for route in relays:
            @pl.when(seq == route[3])
            def _():
                for copy in from_relay(g, route):
                    copy.wait_send()

    for g in range(2):
        for piece in range(pieces):
            for step in range(3):
                out_copy(4 * g + step, g, piece, kvh, kvh).wait_send()
            own_copy(4 * g + 3, g, piece).wait()
            for step in range(1, n_kvh):
                source = lax.rem(kvh + step, n_kvh)
                out_copy(0, g, piece, source, source).wait_recv()


def body(n_chips, n_kvh, queries, keys, values, episode_lengths):
    block = keys.shape[0]
    rows = block // n_kvh
    width = queries.shape[1]
    hbm = pl.BlockSpec(memory_space=pltpu.HBM)
    return pl.pallas_call(
        functools.partial(kernel, n_chips, n_kvh),
        out_shape=pltpu.VMEM((rows, width * n_kvh), jnp.bfloat16),
        in_specs=[hbm, hbm, hbm, hbm],
        out_specs=pl.BlockSpec(memory_space=pl.ANY),
        scratch_shapes=[
            pltpu.SMEM(episode_lengths.shape, jnp.int32),
            pltpu.VMEM((2, GROUP, block, HEAD), jnp.bfloat16),
            pltpu.VMEM((4 * block, 2 * HEAD), jnp.bfloat16),
            pltpu.VMEM((4 * block, 2 * HEAD), jnp.bfloat16),
            pltpu.VMEM((2, block // 2, 2 * HEAD), jnp.bfloat16),
            pltpu.VMEM((2, block, 2 * HEAD), jnp.bfloat16),
            pltpu.VMEM((block, HEAD), jnp.int32),
            pltpu.VMEM((8, rows, GROUP * HEAD), jnp.bfloat16),
            pltpu.SemaphoreType.DMA((13,)),
            pltpu.SemaphoreType.DMA((2, 5)),
            pltpu.SemaphoreType.DMA((2, 3)),
            pltpu.SemaphoreType.DMA((2,)),
            pltpu.SemaphoreType.DMA((2,)),
            pltpu.SemaphoreType.DMA((8, GROUP // STACK)),
            pltpu.SemaphoreType.DMA((2, n_kvh, GROUP // STACK)),
            pltpu.SemaphoreType.DMA((2, GROUP // STACK)),
        ],
        compiler_params=pltpu.CompilerParams(
            collective_id=0, has_side_effects=True, vmem_limit_bytes=40 << 20
        ),
        name="attention",
    )(*(
        pltpu.with_memory_space_constraint(x, pltpu.HBM)
        for x in (episode_lengths, queries, keys, values)
    ))


def solution(mesh):
    return jax.shard_map(
        functools.partial(body, mesh.shape["seq"] // 2, mesh.shape["kvh"]),
        mesh=mesh,
        in_specs=(P("seq", "kvh"), P("seq", "kvh"), P("seq", "kvh"), P()),
        out_specs=P(("seq", "kvh"), None),
        check_vma=False,
    )
```

```python
import functools
import math

import jax
import jax.numpy as jnp
from jax import lax
from jax.experimental import pallas as pl
from jax.experimental.pallas import tpu as pltpu
from jax.sharding import PartitionSpec as P

HEAD = 128
GROUP = 4
WINDOW = 1536
MESH = pl.DeviceIdType.MESH
MASKED = -1e30
STACK = 2


def attend(q, kv_ref, base, begin, scale, finish):
    stack = STACK
    rows = begin.shape[0]
    row = lax.broadcasted_iota(jnp.int32, (rows, rows), 0)
    col = lax.broadcasted_iota(jnp.int32, (rows, rows), 1)
    last = col <= row
    edge_seen = jnp.where(last, col + WINDOW, col) >= begin
    middle_seen = lax.broadcasted_iota(jnp.int32, (rows, WINDOW - rows), 1) + rows >= begin
    last, edge_seen, middle_seen = (
        jnp.concatenate([mask] * stack, 0) for mask in (last, edge_seen, middle_seen)
    )

    def part(offset, count):
        span = pl.ds(base + offset, count)
        return kv_ref[span, 0:HEAD], kv_ref[span, HEAD:2 * HEAD]

    first_k, first_v = part(0, rows)
    middle_k, middle_v = part(rows, WINDOW - rows)
    last_k, last_v = part(WINDOW, rows)

    def score(lhs, keys):
        return lax.dot_general(
            lhs, keys, (((1,), (1,)), ((), ())), preferred_element_type=jnp.float32
        )

    def add_up(weights, values):
        return jnp.dot(weights, values, preferred_element_type=jnp.float32)

    for j in range(0, GROUP, stack):
        lhs = jnp.concatenate(q[j:j + stack], 0)
        edge = jnp.where(last, score(lhs, last_k), score(lhs, first_k))
        edge = jnp.where(edge_seen, edge, MASKED)
        middle = jnp.where(middle_seen, score(lhs, middle_k), MASKED)
        top = jnp.maximum(
            jnp.max(middle, axis=1, keepdims=True), jnp.max(edge, axis=1, keepdims=True)
        )
        edge = jnp.exp2((edge - top) * scale)
        middle = jnp.exp2((middle - top) * scale)
        total = jnp.sum(middle, axis=1, keepdims=True) + jnp.sum(edge, axis=1, keepdims=True)
        edge = edge.astype(jnp.bfloat16)
        none = jnp.zeros_like(edge)
        summed = add_up(middle.astype(jnp.bfloat16), middle_v)
        summed += add_up(jnp.where(last, edge, none), last_v)
        summed += add_up(jnp.where(last, none, edge), first_v)
        out = (summed / total).astype(jnp.bfloat16)
        finish(j // stack, [out[i * rows:(i + 1) * rows] for i in range(stack)])


def crossing(n_seq):
    if n_seq != 128:
        return ()
    return (
        (63, ((64, 2),), 0, 127), (63, ((64, 2),), 1, 79),
        (62, ((64, 1),), 0, None), (62, ((64, 1),), 1, 119),
    )


def back(chip):
    return chip - 1 + 4 * ((3 - chip % 4) // 3)


def around(chip):
    return chip + 1 - 4 * ((chip % 4) // 3)


def targets(n_chips, n_kvh, routes):
    far = {to // 2 for route in routes for to, there in route[1] if there == 0}
    leaves = {(route[0], there) for route in routes for _, there in route[1]}
    sends = [set() for _ in range(2 * n_chips)]
    for chip in range(n_chips):
        sends[2 * chip].add(2 * chip + 1)
        if chip + 1 < n_chips and (2 * chip, 1) not in leaves:
            sends[2 * chip].add(2 * chip + 2)
        if chip + 1 < n_chips and (2 * chip + 1, 2) not in leaves:
            sends[2 * chip + 1].add(2 * chip + 2)
        if chip + 2 < n_chips and chip + 2 not in far:
            by = 2 * back(chip) + 1
            sends[2 * chip + 1].add(by)
            sends[by].add(2 * chip + 4)
    for source, to, _, by in routes:
        reached = {device for device, _ in to}
        if by is None:
            sends[source] |= reached
        else:
            sends[source].add(by)
            sends[by] |= reached
    return [len(s) + n_kvh - 1 for s in sends]


def one_of(seq, devices):
    found = seq == devices[0]
    for device in devices[1:]:
        found = found | (seq == device)
    return found


def kernel(
    n_chips, n_kvh, lengths_hbm, q_hbm, k_hbm, v_hbm, out_ref,
    lengths_ref, q_ref, kv0_ref, kv1_ref, relay_ref, second_ref, start_ref, stage_ref,
    load_sem, kv_send, kv_recv, relay_recv, second_recv, out_send, out_recv, own_sem,
):
    block = k_hbm.shape[0]
    rows = block // n_kvh
    wide = STACK * HEAD
    pieces = GROUP // STACK
    episodes = lengths_ref.shape[0]
    seq = lax.axis_index("seq")
    kvh = lax.axis_index("kvh")
    chip = seq // 2
    first = lax.rem(seq, 2) == 0
    second = lax.rem(seq, 2) == 1
    n_seq = 2 * n_chips
    part = block // 2
    routes = crossing(n_seq)
    relays = [route for route in routes if route[3] is not None]
    scale = math.log2(math.e) / math.sqrt(HEAD)
    kv_refs = (kv0_ref, kv1_ref)

    def slot(g, i):
        return kv_refs[g].at[pl.ds(i * block, block)]

    own = []
    for g in range(2):
        for i, src in enumerate((k_hbm, v_hbm)):
            own.append(pltpu.make_async_copy(
                src.at[:, pl.ds(g * HEAD, HEAD)],
                kv_refs[g].at[pl.ds(3 * block, block), pl.ds(i * HEAD, HEAD)],
                load_sem.at[2 * g + i],
            ))
    later = [pltpu.make_async_copy(lengths_hbm, lengths_ref, load_sem.at[4])]
    for g in range(2):
        for j in range(GROUP):
            later.append(pltpu.make_async_copy(
                q_hbm.at[:, pl.ds((g * GROUP + j) * HEAD, HEAD)],
                q_ref.at[g, j],
                load_sem.at[5 + g * GROUP + j],
            ))
    for copy in own + later:
        copy.start()

    barrier = pltpu.get_barrier_semaphore()

    def greet(s, k):
        pl.semaphore_signal(barrier, inc=1, device_id=(s, k), device_id_type=MESH)

    for step in range(1, n_kvh):
        greet(seq, lax.rem(kvh + step, n_kvh))

    def far(slot_there):
        devices = sorted({to for route in routes for to, there in route[1] if there == slot_there})
        return one_of(seq, devices) if devices else seq < 0

    def leaves(slot_there):
        devices = sorted({r[0] for r in routes for _, there in r[1] if there == slot_there})
        return one_of(seq, devices) if devices else seq < 0

    no = jnp.logical_not
    has_next = chip < n_chips - 1
    has_second = (chip < n_chips - 2) & no(leaves(0))
    sends_second = has_second
    for source in sorted({route[0] for route in routes if route[1][0][1] == 0}):
        sends_second = sends_second | (seq == source)
    gets_second = first & (chip >= 2) & no(far(0))
    aim = around(chip) + 2
    passes = second & (aim < n_chips)
    for device in sorted({to for route in routes for to, there in route[1] if there == 0}):
        passes = passes & (aim != device // 2)

    @pl.when(first & (chip >= 1) & no(far(2)))
    def _():
        greet(seq - 1, kvh)

    @pl.when(first & (chip >= 1) & no(far(1)))
    def _():
        greet(seq - 2, kvh)

    @pl.when(gets_second)
    def _():
        greet(2 * back(chip - 2) + 1, kvh)

    @pl.when(second)
    def _():
        greet(seq - 1, kvh)

    @pl.when(passes)
    def _():
        greet(2 * aim - 3, kvh)

    greeted = set()
    for source, to, _, by in routes:
        pairs = [(device, source if by is None else by) for device, _ in to]
        for receiver, sender in pairs + [(by, source)]:
            if receiver is not None and (receiver, sender) not in greeted:
                greeted.add((receiver, sender))

                @pl.when(seq == receiver)
                def _():
                    greet(sender, kvh)

    counts = targets(n_chips, n_kvh, routes)
    usual = (n_kvh + 1, n_kvh + 2)
    odd_ones = [s for s in range(n_seq) if counts[s] != usual[s % 2]]
    for count in sorted({counts[s] for s in odd_ones}):
        @pl.when(one_of(seq, [s for s in odd_ones if counts[s] == count]))
        def _():
            pl.semaphore_wait(barrier, count)

    for parity in range(2):
        @pl.when((first, second)[parity] & no(one_of(seq, odd_ones)))
        def _():
            pl.semaphore_wait(barrier, usual[parity])

    def send(g, src, dst, to, sem, recv):
        return pltpu.make_async_remote_copy(
            src_ref=src, dst_ref=dst, send_sem=kv_send.at[g, sem], recv_sem=recv,
            device_id=(to, kvh), device_id_type=MESH,
        )

    def pass_slot(g, here, there, by, sem):
        return send(g, slot(g, here), slot(g, there), seq + by, sem, kv_recv.at[g, there])

    def arrived(g, there):
        pass_slot(g, there, there, 1, 0).wait_recv()

    def to_sibling(g):
        return pass_slot(g, 3, 2, 1, 1)

    def to_second(g):
        return send(g, slot(g, 3), second_ref.at[g], 2 * back(chip) + 1, 1, second_recv.at[g])

    def from_second(g):
        return send(g, second_ref.at[g], slot(g, 0), 2 * aim, 3, kv_recv.at[g, 0])

    def rows_of(g, i, piece):
        return kv_refs[g].at[pl.ds(i * block + piece * part, part)]

    def to_relay(g, route, sem):
        return send(g, rows_of(g, 3, route[2]), relay_ref.at[g], route[3], sem, relay_recv.at[g])

    def from_relay(g, route):
        return [
            send(g, relay_ref.at[g], rows_of(g, there, route[2]), to, sem, kv_recv.at[g, there])
            for (to, there), sem in zip(route[1], (2, 4))
        ]

    def cross(g, slots, sem):
        for route in routes:
            source, ((to, there), *_), piece, by = route
            if there not in slots:
                continue

            @pl.when(seq == source)
            def _():
                if by is None:
                    send(
                        g, rows_of(g, 3, piece), rows_of(g, there, piece), to, sem,
                        kv_recv.at[g, there],
                    ).start()
                else:
                    to_relay(g, route, sem).start()

    def to_next(g):
        @pl.when(first & has_next & no(leaves(1)))
        def _():
            pass_slot(g, 3, 1, 2, 0).start()

        @pl.when(second & has_next & no(leaves(2)))
        def _():
            pass_slot(g, 3, 2, 1, 0).start()

        cross(g, (1, 2), 0)

        @pl.when(first)
        def _():
            to_sibling(g).start()

    def next_left(g):
        @pl.when(has_next)
        def _():
            pass_slot(g, 3, 1, 1, 0).wait_send()

    def ahead_second(g):
        @pl.when(second & has_second)
        def _():
            to_second(g).start()
        cross(g, (0,), 1)

    def second_left(g):
        @pl.when(second & sends_second)
        def _():
            to_second(g).wait_send()

    def relay(g):
        for route in relays:
            @pl.when(seq == route[3])
            def _():
                to_relay(g, route, 0).wait_recv()
                for copy in from_relay(g, route):
                    copy.start()

    def relay_second(g):
        @pl.when(passes)
        def _():
            to_second(g).wait_recv()
            from_second(g).start()

    def pass_on(g):
        @pl.when(chip >= 1)
        def _():
            arrived(g, 2)
        pass_slot(g, 2, 1, 1, 2).start()

        @pl.when(chip >= 1)
        def _():
            arrived(g, 1)
        pass_slot(g, 1, 0, 1, 3).start()

    def window_in(g):
        @pl.when(first & (chip >= 2))
        def _():
            arrived(g, 0)

        @pl.when(second)
        def _():
            for i in range(3):
                arrived(g, i)

    for copy in own:
        copy.wait()

    to_next(0)
    ahead_second(0)

    @pl.when(first & (chip == 0))
    def _():
        for ref in kv_refs:
            ref[0:3 * block, :] = jnp.zeros((3 * block, 2 * HEAD), jnp.bfloat16)

    @pl.when(first & (chip == 1))
    def _():
        for ref in kv_refs:
            ref[0:block, :] = jnp.zeros((block, 2 * HEAD), jnp.bfloat16)

    for copy in later:
        copy.wait()
    position = seq * block + lax.broadcasted_iota(jnp.int32, (block, HEAD), 0)
    start_ref[...] = jnp.zeros((block, HEAD), jnp.int32)

    def add_episode(e, end):
        end = end + lengths_ref[e]
        start_ref[...] = jnp.where(position >= end, end, start_ref[...])
        return end

    lax.fori_loop(0, episodes, add_episode, jnp.int32(0))

    def out_columns(k, g, piece):
        return pl.ds(pl.multiple_of(((k * 2 + g) * GROUP + piece * STACK) * HEAD, HEAD), wide)

    def staged(u, piece):
        return stage_ref.at[u, :, pl.ds(piece * wide, wide)]

    def out_copy(u, g, piece, to, source):
        return pltpu.make_async_remote_copy(
            src_ref=staged(u, piece), dst_ref=out_ref.at[:, out_columns(source, g, piece)],
            send_sem=out_send.at[u, piece], recv_sem=out_recv.at[g, source, piece],
            device_id=(seq, to), device_id_type=MESH,
        )

    def own_copy(u, g, piece):
        return pltpu.make_async_copy(
            staged(u, piece), out_ref.at[:, out_columns(kvh, g, piece)], own_sem.at[g, piece]
        )

    def target(step):
        late, odd = step // 2, step % 2
        upper, low = kvh // 2, kvh % 2
        far = (1 - upper) * (3 - odd) + upper * odd
        near = 2 * upper + (1 - low) * (1 - odd) + low * odd
        return (1 - late) * far + late * near

    def unit(g, step):
        r = target(step)
        u = 4 * g + step
        base = pl.multiple_of(r * rows, rows)
        begin = start_ref[pl.ds(base, rows), 0:1] - (seq * block - WINDOW + base)
        q = [q_ref[g, j, pl.ds(base, rows), :] for j in range(GROUP)]

        def finish(piece, outs):
            for j in range(STACK):
                at = (piece * STACK + j) * HEAD
                stage_ref[u, :, at:at + HEAD] = outs[j]

            @pl.when(step < 3)
            def _():
                out_copy(u, g, piece, r, kvh).start()

            @pl.when(step == 3)
            def _():
                own_copy(u, g, piece).start()

        attend(q, kv_refs[g], base, begin, scale, finish)

    sources = sorted({route[0] for route in routes})
    early = one_of(seq, sources) if sources else seq < 0

    @pl.when(early)
    def _():
        next_left(0)
        to_next(1)
        second_left(0)
        ahead_second(1)
    relay(0)
    relay_second(0)

    @pl.when(no(early))
    def _():
        next_left(0)
        to_next(1)

    @pl.when(first)
    def _():
        pass_on(0)

    @pl.when(no(early))
    def _():
        second_left(0)
        ahead_second(1)
    window_in(0)

    @pl.loop(0, 4)
    def _(step):
        @pl.when(step == 1)
        def _():
            relay(1)
            relay_second(1)

        @pl.when(first & (step == 2))
        def _():
            pass_on(1)

        unit(0, step)

    window_in(1)

    @pl.loop(0, 4)
    def _(step):
        unit(1, step)

    next_left(1)
    second_left(1)
    for g in range(2):
        @pl.when(first)
        def _():
            for sem in range(1, 4):
                pass_slot(g, 3, 2, 1, sem).wait_send()

        @pl.when(passes)
        def _():
            from_second(g).wait_send()
        for route in relays:
            @pl.when(seq == route[3])
            def _():
                for copy in from_relay(g, route):
                    copy.wait_send()

    for g in range(2):
        for piece in range(pieces):
            for step in range(3):
                out_copy(4 * g + step, g, piece, kvh, kvh).wait_send()
            own_copy(4 * g + 3, g, piece).wait()
            for step in range(1, n_kvh):
                source = lax.rem(kvh + step, n_kvh)
                out_copy(0, g, piece, source, source).wait_recv()


def body(n_chips, n_kvh, queries, keys, values, episode_lengths):
    block = keys.shape[0]
    rows = block // n_kvh
    width = queries.shape[1]
    hbm = pl.BlockSpec(memory_space=pltpu.HBM)
    return pl.pallas_call(
        functools.partial(kernel, n_chips, n_kvh),
        out_shape=pltpu.VMEM((rows, width * n_kvh), jnp.bfloat16),
        in_specs=[hbm, hbm, hbm, hbm],
        out_specs=pl.BlockSpec(memory_space=pl.ANY),
        scratch_shapes=[
            pltpu.SMEM(episode_lengths.shape, jnp.int32),
            pltpu.VMEM((2, GROUP, block, HEAD), jnp.bfloat16),
            pltpu.VMEM((4 * block, 2 * HEAD), jnp.bfloat16),
            pltpu.VMEM((4 * block, 2 * HEAD), jnp.bfloat16),
            pltpu.VMEM((2, block // 2, 2 * HEAD), jnp.bfloat16),
            pltpu.VMEM((2, block, 2 * HEAD), jnp.bfloat16),
            pltpu.VMEM((block, HEAD), jnp.int32),
            pltpu.VMEM((8, rows, GROUP * HEAD), jnp.bfloat16),
            pltpu.SemaphoreType.DMA((13,)),
            pltpu.SemaphoreType.DMA((2, 5)),
            pltpu.SemaphoreType.DMA((2, 3)),
            pltpu.SemaphoreType.DMA((2,)),
            pltpu.SemaphoreType.DMA((2,)),
            pltpu.SemaphoreType.DMA((8, GROUP // STACK)),
            pltpu.SemaphoreType.DMA((2, n_kvh, GROUP // STACK)),
            pltpu.SemaphoreType.DMA((2, GROUP // STACK)),
        ],
        compiler_params=pltpu.CompilerParams(
            collective_id=0, has_side_effects=True, vmem_limit_bytes=40 << 20
        ),
        name="attention",
    )(*(
        pltpu.with_memory_space_constraint(x, pltpu.HBM)
        for x in (episode_lengths, queries, keys, values)
    ))


def solution(mesh):
    return jax.shard_map(
        functools.partial(body, mesh.shape["seq"] // 2, mesh.shape["kvh"]),
        mesh=mesh,
        in_specs=(P("seq", "kvh"), P("seq", "kvh"), P("seq", "kvh"), P()),
        out_specs=P(("seq", "kvh"), None),
        check_vma=False,
    )
```

```python
import functools
import math

import jax
import jax.numpy as jnp
from jax import lax
from jax.experimental import pallas as pl
from jax.experimental.pallas import tpu as pltpu
from jax.sharding import PartitionSpec as P

HEAD = 128
GROUP = 4
WINDOW = 1536
MESH = pl.DeviceIdType.MESH
MASKED = -1e30
STACK = 2


def attend(q, kv_ref, base, begin, scale, finish):
    stack = STACK
    rows = begin.shape[0]
    row = lax.broadcasted_iota(jnp.int32, (rows, rows), 0)
    col = lax.broadcasted_iota(jnp.int32, (rows, rows), 1)
    last = col <= row
    edge_seen = jnp.where(last, col + WINDOW, col) >= begin
    middle_seen = lax.broadcasted_iota(jnp.int32, (rows, WINDOW - rows), 1) + rows >= begin
    last, edge_seen, middle_seen = (
        jnp.concatenate([mask] * stack, 0) for mask in (last, edge_seen, middle_seen)
    )

    def part(offset, count):
        span = pl.ds(base + offset, count)
        return kv_ref[span, 0:HEAD], kv_ref[span, HEAD:2 * HEAD]

    first_k, first_v = part(0, rows)
    middle_k, middle_v = part(rows, WINDOW - rows)
    last_k, last_v = part(WINDOW, rows)

    def score(lhs, keys):
        return lax.dot_general(
            lhs, keys, (((1,), (1,)), ((), ())), preferred_element_type=jnp.float32
        )

    def add_up(weights, values):
        return jnp.dot(weights, values, preferred_element_type=jnp.float32)

    for j in range(0, GROUP, stack):
        lhs = jnp.concatenate(q[j:j + stack], 0)
        edge = jnp.where(last, score(lhs, last_k), score(lhs, first_k))
        edge = jnp.where(edge_seen, edge, MASKED)
        middle = jnp.where(middle_seen, score(lhs, middle_k), MASKED)
        top = jnp.maximum(
            jnp.max(middle, axis=1, keepdims=True), jnp.max(edge, axis=1, keepdims=True)
        )
        edge = jnp.exp2((edge - top) * scale)
        middle = jnp.exp2((middle - top) * scale)
        total = jnp.sum(middle, axis=1, keepdims=True) + jnp.sum(edge, axis=1, keepdims=True)
        edge = edge.astype(jnp.bfloat16)
        none = jnp.zeros_like(edge)
        summed = add_up(middle.astype(jnp.bfloat16), middle_v)
        summed += add_up(jnp.where(last, edge, none), last_v)
        summed += add_up(jnp.where(last, none, edge), first_v)
        out = (summed / total).astype(jnp.bfloat16)
        finish(j // stack, [out[i * rows:(i + 1) * rows] for i in range(stack)])


def crossing(n_seq):
    if n_seq != 128:
        return ()
    return (
        (63, ((64, 2),), 0, 127), (63, ((64, 2),), 1, 79),
        (62, ((64, 1),), 0, None), (62, ((64, 1),), 1, 119),
    )


def detours(n_seq):
    return ((64, 65), 8) if n_seq == 128 else ((), 0)


def back(chip):
    return chip - 1 + 4 * ((3 - chip % 4) // 3)


def around(chip):
    return chip + 1 - 4 * ((chip % 4) // 3)


def targets(n_chips, n_kvh, routes):
    far = {to // 2 for route in routes for to, there in route[1] if there == 0}
    leaves = {(route[0], there) for route in routes for _, there in route[1]}
    sends = [set() for _ in range(2 * n_chips)]
    for chip in range(n_chips):
        sends[2 * chip].add(2 * chip + 1)
        if chip + 1 < n_chips and (2 * chip, 1) not in leaves:
            sends[2 * chip].add(2 * chip + 2)
        if chip + 1 < n_chips and (2 * chip + 1, 2) not in leaves:
            sends[2 * chip + 1].add(2 * chip + 2)
        if chip + 2 < n_chips and chip + 2 not in far:
            by = 2 * back(chip) + 1
            sends[2 * chip + 1].add(by)
            sends[by].add(2 * chip + 4)
    for source, to, _, by in routes:
        reached = {device for device, _ in to}
        if by is None:
            sends[source] |= reached
        else:
            sends[source].add(by)
            sends[by] |= reached
    late, aside = detours(2 * n_chips)
    for device in late:
        sends[device].add(device + aside)
        sends[device + aside].add(device)
    return [len(s) + n_kvh - 1 for s in sends]


def one_of(seq, devices):
    found = seq == devices[0]
    for device in devices[1:]:
        found = found | (seq == device)
    return found


def kernel(
    n_chips, n_kvh, lengths_hbm, q_hbm, k_hbm, v_hbm, out_ref,
    lengths_ref, q_ref, kv0_ref, kv1_ref, relay_ref, second_ref, carry_ref, start_ref, stage_ref,
    load_sem, kv_send, kv_recv, relay_recv, second_recv, carry_send, carry_recv, out_send, out_recv, own_sem,
):
    block = k_hbm.shape[0]
    rows = block // n_kvh
    wide = STACK * HEAD
    pieces = GROUP // STACK
    episodes = lengths_ref.shape[0]
    seq = lax.axis_index("seq")
    kvh = lax.axis_index("kvh")
    chip = seq // 2
    first = lax.rem(seq, 2) == 0
    second = lax.rem(seq, 2) == 1
    n_seq = 2 * n_chips
    part = block // 2
    routes = crossing(n_seq)
    relays = [route for route in routes if route[3] is not None]
    scale = math.log2(math.e) / math.sqrt(HEAD)
    kv_refs = (kv0_ref, kv1_ref)

    def slot(g, i):
        return kv_refs[g].at[pl.ds(i * block, block)]

    own = []
    for g in range(2):
        for i, src in enumerate((k_hbm, v_hbm)):
            own.append(pltpu.make_async_copy(
                src.at[:, pl.ds(g * HEAD, HEAD)],
                kv_refs[g].at[pl.ds(3 * block, block), pl.ds(i * HEAD, HEAD)],
                load_sem.at[2 * g + i],
            ))
    later = [pltpu.make_async_copy(lengths_hbm, lengths_ref, load_sem.at[4])]
    for g in range(2):
        for j in range(GROUP):
            later.append(pltpu.make_async_copy(
                q_hbm.at[:, pl.ds((g * GROUP + j) * HEAD, HEAD)],
                q_ref.at[g, j],
                load_sem.at[5 + g * GROUP + j],
            ))
    for copy in own + later:
        copy.start()

    barrier = pltpu.get_barrier_semaphore()

    def greet(s, k):
        pl.semaphore_signal(barrier, inc=1, device_id=(s, k), device_id_type=MESH)

    for step in range(1, n_kvh):
        greet(seq, lax.rem(kvh + step, n_kvh))

    def far(slot_there):
        devices = sorted({to for route in routes for to, there in route[1] if there == slot_there})
        return one_of(seq, devices) if devices else seq < 0

    def leaves(slot_there):
        devices = sorted({r[0] for r in routes for _, there in r[1] if there == slot_there})
        return one_of(seq, devices) if devices else seq < 0

    no = jnp.logical_not
    has_next = chip < n_chips - 1
    has_second = (chip < n_chips - 2) & no(leaves(0))
    sends_second = has_second
    for source in sorted({route[0] for route in routes if route[1][0][1] == 0}):
        sends_second = sends_second | (seq == source)
    gets_second = first & (chip >= 2) & no(far(0))
    aim = around(chip) + 2
    passes = second & (aim < n_chips)
    for device in sorted({to for route in routes for to, there in route[1] if there == 0}):
        passes = passes & (aim != device // 2)

    @pl.when(first & (chip >= 1) & no(far(2)))
    def _():
        greet(seq - 1, kvh)

    @pl.when(first & (chip >= 1) & no(far(1)))
    def _():
        greet(seq - 2, kvh)

    @pl.when(gets_second)
    def _():
        greet(2 * back(chip - 2) + 1, kvh)

    @pl.when(second)
    def _():
        greet(seq - 1, kvh)

    @pl.when(passes)
    def _():
        greet(2 * aim - 3, kvh)

    greeted = set()
    for source, to, _, by in routes:
        pairs = [(device, source if by is None else by) for device, _ in to]
        for receiver, sender in pairs + [(by, source)]:
            if receiver is not None and (receiver, sender) not in greeted:
                greeted.add((receiver, sender))

                @pl.when(seq == receiver)
                def _():
                    greet(sender, kvh)

    late, aside = detours(n_seq)
    leaving = one_of(seq, late) if late else seq < 0
    carrying = one_of(seq, [device + aside for device in late]) if late else seq < 0
    outer = (kvh == 0) | (kvh == n_kvh - 1)
    if late:
        @pl.when(leaving)
        def _():
            greet(seq + aside, kvh)

        for low in range(2):
            @pl.when(carrying & outer)
            def _():
                greet(seq - aside, (3 - kvh) // 3 * 2 + low)

    counts = targets(n_chips, n_kvh, routes)
    usual = (n_kvh + 1, n_kvh + 2)
    odd_ones = [s for s in range(n_seq) if counts[s] != usual[s % 2]]
    for count in sorted({counts[s] for s in odd_ones}):
        @pl.when(one_of(seq, [s for s in odd_ones if counts[s] == count]))
        def _():
            pl.semaphore_wait(barrier, count)

    for parity in range(2):
        @pl.when((first, second)[parity] & no(one_of(seq, odd_ones)))
        def _():
            pl.semaphore_wait(barrier, usual[parity])

    def send(g, src, dst, to, sem, recv):
        return pltpu.make_async_remote_copy(
            src_ref=src, dst_ref=dst, send_sem=kv_send.at[g, sem], recv_sem=recv,
            device_id=(to, kvh), device_id_type=MESH,
        )

    def pass_slot(g, here, there, by, sem):
        return send(g, slot(g, here), slot(g, there), seq + by, sem, kv_recv.at[g, there])

    def arrived(g, there):
        pass_slot(g, there, there, 1, 0).wait_recv()

    def to_sibling(g):
        return pass_slot(g, 3, 2, 1, 1)

    def to_second(g):
        return send(g, slot(g, 3), second_ref.at[g], 2 * back(chip) + 1, 1, second_recv.at[g])

    def from_second(g):
        return send(g, second_ref.at[g], slot(g, 0), 2 * aim, 3, kv_recv.at[g, 0])

    def rows_of(g, i, piece):
        return kv_refs[g].at[pl.ds(i * block + piece * part, part)]

    def to_relay(g, route, sem):
        return send(g, rows_of(g, 3, route[2]), relay_ref.at[g], route[3], sem, relay_recv.at[g])

    def from_relay(g, route):
        return [
            send(g, relay_ref.at[g], rows_of(g, there, route[2]), to, sem, kv_recv.at[g, there])
            for (to, there), sem in zip(route[1], (2, 4))
        ]

    def cross(g, slots, sem):
        for route in routes:
            source, ((to, there), *_), piece, by = route
            if there not in slots:
                continue

            @pl.when(seq == source)
            def _():
                if by is None:
                    send(
                        g, rows_of(g, 3, piece), rows_of(g, there, piece), to, sem,
                        kv_recv.at[g, there],
                    ).start()
                else:
                    to_relay(g, route, sem).start()

    def to_next(g):
        @pl.when(first & has_next & no(leaves(1)))
        def _():
            pass_slot(g, 3, 1, 2, 0).start()

        @pl.when(second & has_next & no(leaves(2)))
        def _():
            pass_slot(g, 3, 2, 1, 0).start()

        cross(g, (1, 2), 0)

        @pl.when(first)
        def _():
            to_sibling(g).start()

    def next_left(g):
        @pl.when(has_next)
        def _():
            pass_slot(g, 3, 1, 1, 0).wait_send()

    def ahead_second(g):
        @pl.when(second & has_second)
        def _():
            to_second(g).start()
        cross(g, (0,), 1)

    def second_left(g):
        @pl.when(second & sends_second)
        def _():
            to_second(g).wait_send()

    def relay(g):
        for route in relays:
            @pl.when(seq == route[3])
            def _():
                to_relay(g, route, 0).wait_recv()
                for copy in from_relay(g, route):
                    copy.start()

    def relay_second(g):
        @pl.when(passes)
        def _():
            to_second(g).wait_recv()
            from_second(g).start()

    def pass_on(g):
        @pl.when(chip >= 1)
        def _():
            arrived(g, 2)
        pass_slot(g, 2, 1, 1, 2).start()

        @pl.when(chip >= 1)
        def _():
            arrived(g, 1)
        pass_slot(g, 1, 0, 1, 3).start()

    def window_in(g):
        @pl.when(first & (chip >= 2))
        def _():
            arrived(g, 0)

        @pl.when(second)
        def _():
            for i in range(3):
                arrived(g, i)

    for copy in own:
        copy.wait()

    to_next(0)
    ahead_second(0)

    @pl.when(first & (chip == 0))
    def _():
        for ref in kv_refs:
            ref[0:3 * block, :] = jnp.zeros((3 * block, 2 * HEAD), jnp.bfloat16)

    @pl.when(first & (chip == 1))
    def _():
        for ref in kv_refs:
            ref[0:block, :] = jnp.zeros((block, 2 * HEAD), jnp.bfloat16)

    for copy in later:
        copy.wait()
    position = seq * block + lax.broadcasted_iota(jnp.int32, (block, HEAD), 0)
    start_ref[...] = jnp.zeros((block, HEAD), jnp.int32)

    def add_episode(e, end):
        end = end + lengths_ref[e]
        start_ref[...] = jnp.where(position >= end, end, start_ref[...])
        return end

    lax.fori_loop(0, episodes, add_episode, jnp.int32(0))

    def out_columns(k, g, piece):
        return pl.ds(pl.multiple_of(((k * 2 + g) * GROUP + piece * STACK) * HEAD, HEAD), wide)

    def staged(u, piece):
        return stage_ref.at[u, :, pl.ds(piece * wide, wide)]

    def out_copy(u, g, piece, to, source):
        return pltpu.make_async_remote_copy(
            src_ref=staged(u, piece), dst_ref=out_ref.at[:, out_columns(source, g, piece)],
            send_sem=out_send.at[u, piece], recv_sem=out_recv.at[g, source, piece],
            device_id=(seq, to), device_id_type=MESH,
        )

    def aside_copy(u, piece, to, low):
        return pltpu.make_async_remote_copy(
            src_ref=staged(u, piece), dst_ref=carry_ref.at[low, piece],
            send_sem=out_send.at[u, piece], recv_sem=carry_recv.at[low, piece],
            device_id=(seq + aside, to), device_id_type=MESH,
        )

    def carried_copy(low, piece):
        source = (3 - kvh) // 3 * 2 + low
        return pltpu.make_async_remote_copy(
            src_ref=carry_ref.at[low, piece], dst_ref=out_ref.at[:, out_columns(source, 1, piece)],
            send_sem=carry_send.at[low, piece], recv_sem=out_recv.at[1, source, piece],
            device_id=(seq - aside, kvh), device_id_type=MESH,
        )

    def own_copy(u, g, piece):
        return pltpu.make_async_copy(
            staged(u, piece), out_ref.at[:, out_columns(kvh, g, piece)], own_sem.at[g, piece]
        )

    def target(step):
        late, odd = step // 2, step % 2
        upper, low = kvh // 2, kvh % 2
        far = (1 - upper) * (3 - odd) + upper * odd
        near = 2 * upper + (1 - low) * (1 - odd) + low * odd
        return (1 - late) * far + late * near

    def unit(g, step):
        r = target(step)
        u = 4 * g + step
        base = pl.multiple_of(r * rows, rows)
        begin = start_ref[pl.ds(base, rows), 0:1] - (seq * block - WINDOW + base)
        q = [q_ref[g, j, pl.ds(base, rows), :] for j in range(GROUP)]

        def finish(piece, outs):
            for j in range(STACK):
                at = (piece * STACK + j) * HEAD
                stage_ref[u, :, at:at + HEAD] = outs[j]

            on_side = leaving & (step == 0) if g == 1 and late else None

            @pl.when(step < 3 if on_side is None else (step < 3) & no(on_side))
            def _():
                out_copy(u, g, piece, r, kvh).start()

            if on_side is not None:
                @pl.when(on_side)
                def _():
                    aside_copy(u, piece, r, kvh % 2).start()

            @pl.when(step == 3)
            def _():
                own_copy(u, g, piece).start()

        attend(q, kv_refs[g], base, begin, scale, finish)

    sources = sorted({route[0] for route in routes})
    early = one_of(seq, sources) if sources else seq < 0

    @pl.when(early)
    def _():
        next_left(0)
        to_next(1)
        second_left(0)
        ahead_second(1)
    relay(0)
    relay_second(0)

    @pl.when(no(early))
    def _():
        next_left(0)
        to_next(1)

    @pl.when(first)
    def _():
        pass_on(0)

    @pl.when(no(early))
    def _():
        second_left(0)
        ahead_second(1)
    window_in(0)

    @pl.loop(0, 4)
    def _(step):
        @pl.when(step == 1)
        def _():
            relay(1)
            relay_second(1)

        @pl.when(first & (step == 2))
        def _():
            pass_on(1)

        unit(0, step)

    window_in(1)

    @pl.loop(0, 4)
    def _(step):
        unit(1, step)

    if late:
        @pl.when(carrying & outer)
        def _():
            for low in range(2):
                for piece in range(pieces):
                    aside_copy(0, piece, kvh, low).wait_recv()
                    carried_copy(low, piece).start()
            for low in range(2):
                for piece in range(pieces):
                    carried_copy(low, piece).wait_send()

    next_left(1)
    second_left(1)
    for g in range(2):
        @pl.when(first)
        def _():
            for sem in range(1, 4):
                pass_slot(g, 3, 2, 1, sem).wait_send()

        @pl.when(passes)
        def _():
            from_second(g).wait_send()
        for route in relays:
            @pl.when(seq == route[3])
            def _():
                for copy in from_relay(g, route):
                    copy.wait_send()

    for g in range(2):
        for piece in range(pieces):
            for step in range(3):
                out_copy(4 * g + step, g, piece, kvh, kvh).wait_send()
            own_copy(4 * g + 3, g, piece).wait()
            for step in range(1, n_kvh):
                source = lax.rem(kvh + step, n_kvh)
                out_copy(0, g, piece, source, source).wait_recv()


def body(n_chips, n_kvh, queries, keys, values, episode_lengths):
    block = keys.shape[0]
    rows = block // n_kvh
    width = queries.shape[1]
    hbm = pl.BlockSpec(memory_space=pltpu.HBM)
    return pl.pallas_call(
        functools.partial(kernel, n_chips, n_kvh),
        out_shape=pltpu.VMEM((rows, width * n_kvh), jnp.bfloat16),
        in_specs=[hbm, hbm, hbm, hbm],
        out_specs=pl.BlockSpec(memory_space=pl.ANY),
        scratch_shapes=[
            pltpu.SMEM(episode_lengths.shape, jnp.int32),
            pltpu.VMEM((2, GROUP, block, HEAD), jnp.bfloat16),
            pltpu.VMEM((4 * block, 2 * HEAD), jnp.bfloat16),
            pltpu.VMEM((4 * block, 2 * HEAD), jnp.bfloat16),
            pltpu.VMEM((2, block // 2, 2 * HEAD), jnp.bfloat16),
            pltpu.VMEM((2, block, 2 * HEAD), jnp.bfloat16),
            pltpu.VMEM((2, GROUP // STACK, rows, STACK * HEAD), jnp.bfloat16),
            pltpu.VMEM((block, HEAD), jnp.int32),
            pltpu.VMEM((8, rows, GROUP * HEAD), jnp.bfloat16),
            pltpu.SemaphoreType.DMA((13,)),
            pltpu.SemaphoreType.DMA((2, 5)),
            pltpu.SemaphoreType.DMA((2, 3)),
            pltpu.SemaphoreType.DMA((2,)),
            pltpu.SemaphoreType.DMA((2,)),
            pltpu.SemaphoreType.DMA((2, GROUP // STACK)),
            pltpu.SemaphoreType.DMA((2, GROUP // STACK)),
            pltpu.SemaphoreType.DMA((8, GROUP // STACK)),
            pltpu.SemaphoreType.DMA((2, n_kvh, GROUP // STACK)),
            pltpu.SemaphoreType.DMA((2, GROUP // STACK)),
        ],
        compiler_params=pltpu.CompilerParams(
            collective_id=0, has_side_effects=True, vmem_limit_bytes=40 << 20
        ),
        name="attention",
    )(*(
        pltpu.with_memory_space_constraint(x, pltpu.HBM)
        for x in (episode_lengths, queries, keys, values)
    ))


def solution(mesh):
    return jax.shard_map(
        functools.partial(body, mesh.shape["seq"] // 2, mesh.shape["kvh"]),
        mesh=mesh,
        in_specs=(P("seq", "kvh"), P("seq", "kvh"), P("seq", "kvh"), P()),
        out_specs=P(("seq", "kvh"), None),
        check_vma=False,
    )
```

```python
import functools
import math

import jax
import jax.numpy as jnp
from jax import lax
from jax.experimental import pallas as pl
from jax.experimental.pallas import tpu as pltpu
from jax.sharding import PartitionSpec as P

HEAD = 128
GROUP = 4
WINDOW = 1536
MESH = pl.DeviceIdType.MESH
MASKED = -1e30
STACK = 2


def attend(q, kv_ref, base, begin, scale, finish):
    stack = STACK
    rows = begin.shape[0]
    row = lax.broadcasted_iota(jnp.int32, (rows, rows), 0)
    col = lax.broadcasted_iota(jnp.int32, (rows, rows), 1)
    last = col <= row
    edge_seen = jnp.where(last, col + WINDOW, col) >= begin
    middle_seen = lax.broadcasted_iota(jnp.int32, (rows, WINDOW - rows), 1) + rows >= begin
    last, edge_seen, middle_seen = (
        jnp.concatenate([mask] * stack, 0) for mask in (last, edge_seen, middle_seen)
    )

    def part(offset, count):
        span = pl.ds(base + offset, count)
        return kv_ref[span, 0:HEAD], kv_ref[span, HEAD:2 * HEAD]

    first_k, first_v = part(0, rows)
    middle_k, middle_v = part(rows, WINDOW - rows)
    last_k, last_v = part(WINDOW, rows)

    def score(lhs, keys):
        return lax.dot_general(
            lhs, keys, (((1,), (1,)), ((), ())), preferred_element_type=jnp.float32
        )

    def add_up(weights, values):
        return jnp.dot(weights, values, preferred_element_type=jnp.float32)

    for j in range(0, GROUP, stack):
        lhs = jnp.concatenate(q[j:j + stack], 0)
        edge = jnp.where(last, score(lhs, last_k), score(lhs, first_k))
        edge = jnp.where(edge_seen, edge, MASKED)
        middle = jnp.where(middle_seen, score(lhs, middle_k), MASKED)
        top = jnp.maximum(
            jnp.max(middle, axis=1, keepdims=True), jnp.max(edge, axis=1, keepdims=True)
        )
        edge = jnp.exp2((edge - top) * scale)
        middle = jnp.exp2((middle - top) * scale)
        total = jnp.sum(middle, axis=1, keepdims=True) + jnp.sum(edge, axis=1, keepdims=True)
        edge = edge.astype(jnp.bfloat16)
        none = jnp.zeros_like(edge)
        summed = add_up(middle.astype(jnp.bfloat16), middle_v)
        summed += add_up(jnp.where(last, edge, none), last_v)
        summed += add_up(jnp.where(last, none, edge), first_v)
        out = (summed / total).astype(jnp.bfloat16)
        finish(j // stack, [out[i * rows:(i + 1) * rows] for i in range(stack)])


def crossing(n_seq):
    if n_seq != 128:
        return ()
    return (
        (63, ((64, 2), (66, 0)), 0, 127), (63, ((64, 2), (66, 0)), 1, 79),
        (62, ((64, 1),), 0, None), (62, ((64, 1),), 1, 119),
        (61, ((64, 0),), 0, 123), (61, ((64, 0),), 1, 125),
    )


def detours(n_seq):
    return ((64, 65), 8) if n_seq == 128 else ((), 0)


def back(chip):
    return chip - 1 + 4 * ((3 - chip % 4) // 3)


def around(chip):
    return chip + 1 - 4 * ((chip % 4) // 3)


def targets(n_chips, n_kvh, routes):
    far = {to // 2 for route in routes for to, there in route[1] if there == 0}
    leaves = {(route[0], there) for route in routes for _, there in route[1]}
    sends = [set() for _ in range(2 * n_chips)]
    for chip in range(n_chips):
        sends[2 * chip].add(2 * chip + 1)
        if chip + 1 < n_chips and (2 * chip, 1) not in leaves:
            sends[2 * chip].add(2 * chip + 2)
        if chip + 1 < n_chips and (2 * chip + 1, 2) not in leaves:
            sends[2 * chip + 1].add(2 * chip + 2)
        if chip + 2 < n_chips and chip + 2 not in far:
            by = 2 * back(chip) + 1
            sends[2 * chip + 1].add(by)
            sends[by].add(2 * chip + 4)
    for source, to, _, by in routes:
        reached = {device for device, _ in to}
        if by is None:
            sends[source] |= reached
        else:
            sends[source].add(by)
            sends[by] |= reached
    late, aside = detours(2 * n_chips)
    for device in late:
        sends[device].add(device + aside)
        sends[device + aside].add(device)
    return [len(s) + n_kvh - 1 for s in sends]


def one_of(seq, devices):
    found = seq == devices[0]
    for device in devices[1:]:
        found = found | (seq == device)
    return found


def kernel(
    n_chips, n_kvh, lengths_hbm, q_hbm, k_hbm, v_hbm, out_ref,
    lengths_ref, q_ref, kv0_ref, kv1_ref, relay_ref, second_ref, carry_ref, start_ref, stage_ref,
    load_sem, kv_send, kv_recv, relay_recv, second_recv, carry_send, carry_recv, out_send, out_recv, own_sem,
):
    block = k_hbm.shape[0]
    rows = block // n_kvh
    wide = STACK * HEAD
    pieces = GROUP // STACK
    episodes = lengths_ref.shape[0]
    seq = lax.axis_index("seq")
    kvh = lax.axis_index("kvh")
    chip = seq // 2
    first = lax.rem(seq, 2) == 0
    second = lax.rem(seq, 2) == 1
    n_seq = 2 * n_chips
    part = block // 2
    routes = crossing(n_seq)
    relays = [route for route in routes if route[3] is not None]
    scale = math.log2(math.e) / math.sqrt(HEAD)
    kv_refs = (kv0_ref, kv1_ref)

    def slot(g, i):
        return kv_refs[g].at[pl.ds(i * block, block)]

    own = []
    for g in range(2):
        for i, src in enumerate((k_hbm, v_hbm)):
            own.append(pltpu.make_async_copy(
                src.at[:, pl.ds(g * HEAD, HEAD)],
                kv_refs[g].at[pl.ds(3 * block, block), pl.ds(i * HEAD, HEAD)],
                load_sem.at[2 * g + i],
            ))
    later = [pltpu.make_async_copy(lengths_hbm, lengths_ref, load_sem.at[4])]
    for g in range(2):
        for j in range(GROUP):
            later.append(pltpu.make_async_copy(
                q_hbm.at[:, pl.ds((g * GROUP + j) * HEAD, HEAD)],
                q_ref.at[g, j],
                load_sem.at[5 + g * GROUP + j],
            ))
    for copy in own + later:
        copy.start()

    barrier = pltpu.get_barrier_semaphore()

    def greet(s, k):
        pl.semaphore_signal(barrier, inc=1, device_id=(s, k), device_id_type=MESH)

    for step in range(1, n_kvh):
        greet(seq, lax.rem(kvh + step, n_kvh))

    def far(slot_there):
        devices = sorted({to for route in routes for to, there in route[1] if there == slot_there})
        return one_of(seq, devices) if devices else seq < 0

    def leaves(slot_there):
        devices = sorted({r[0] for r in routes for _, there in r[1] if there == slot_there})
        return one_of(seq, devices) if devices else seq < 0

    no = jnp.logical_not
    has_next = chip < n_chips - 1
    has_second = (chip < n_chips - 2) & no(leaves(0))
    sends_second = has_second
    for source in sorted({route[0] for route in routes if route[1][0][1] == 0}):
        sends_second = sends_second | (seq == source)
    gets_second = first & (chip >= 2) & no(far(0))
    aim = around(chip) + 2
    passes = second & (aim < n_chips)
    for device in sorted({to for route in routes for to, there in route[1] if there == 0}):
        passes = passes & (aim != device // 2)

    @pl.when(first & (chip >= 1) & no(far(2)))
    def _():
        greet(seq - 1, kvh)

    @pl.when(first & (chip >= 1) & no(far(1)))
    def _():
        greet(seq - 2, kvh)

    @pl.when(gets_second)
    def _():
        greet(2 * back(chip - 2) + 1, kvh)

    @pl.when(second)
    def _():
        greet(seq - 1, kvh)

    @pl.when(passes)
    def _():
        greet(2 * aim - 3, kvh)

    greeted = set()
    for source, to, _, by in routes:
        pairs = [(device, source if by is None else by) for device, _ in to]
        for receiver, sender in pairs + [(by, source)]:
            if receiver is not None and (receiver, sender) not in greeted:
                greeted.add((receiver, sender))

                @pl.when(seq == receiver)
                def _():
                    greet(sender, kvh)

    late, aside = detours(n_seq)
    leaving = one_of(seq, late) if late else seq < 0
    carrying = one_of(seq, [device + aside for device in late]) if late else seq < 0
    outer = (kvh == 0) | (kvh == n_kvh - 1)
    if late:
        @pl.when(leaving)
        def _():
            greet(seq + aside, kvh)

        for low in range(2):
            @pl.when(carrying & outer)
            def _():
                greet(seq - aside, (3 - kvh) // 3 * 2 + low)

    counts = targets(n_chips, n_kvh, routes)
    usual = (n_kvh + 1, n_kvh + 2)
    odd_ones = [s for s in range(n_seq) if counts[s] != usual[s % 2]]
    for count in sorted({counts[s] for s in odd_ones}):
        @pl.when(one_of(seq, [s for s in odd_ones if counts[s] == count]))
        def _():
            pl.semaphore_wait(barrier, count)

    for parity in range(2):
        @pl.when((first, second)[parity] & no(one_of(seq, odd_ones)))
        def _():
            pl.semaphore_wait(barrier, usual[parity])

    def send(g, src, dst, to, sem, recv):
        return pltpu.make_async_remote_copy(
            src_ref=src, dst_ref=dst, send_sem=kv_send.at[g, sem], recv_sem=recv,
            device_id=(to, kvh), device_id_type=MESH,
        )

    def pass_slot(g, here, there, by, sem):
        return send(g, slot(g, here), slot(g, there), seq + by, sem, kv_recv.at[g, there])

    def arrived(g, there):
        pass_slot(g, there, there, 1, 0).wait_recv()

    def to_sibling(g):
        return pass_slot(g, 3, 2, 1, 1)

    def to_second(g):
        return send(g, slot(g, 3), second_ref.at[g], 2 * back(chip) + 1, 1, second_recv.at[g])

    def from_second(g):
        return send(g, second_ref.at[g], slot(g, 0), 2 * aim, 3, kv_recv.at[g, 0])

    def rows_of(g, i, piece):
        return kv_refs[g].at[pl.ds(i * block + piece * part, part)]

    def to_relay(g, route, sem):
        return send(g, rows_of(g, 3, route[2]), relay_ref.at[g], route[3], sem, relay_recv.at[g])

    def from_relay(g, route):
        return [
            send(g, relay_ref.at[g], rows_of(g, there, route[2]), to, sem, kv_recv.at[g, there])
            for (to, there), sem in zip(route[1], (2, 4))
        ]

    def cross(g, slots, sem):
        for route in routes:
            source, ((to, there), *_), piece, by = route
            if there not in slots:
                continue

            @pl.when(seq == source)
            def _():
                if by is None:
                    send(
                        g, rows_of(g, 3, piece), rows_of(g, there, piece), to, sem,
                        kv_recv.at[g, there],
                    ).start()
                else:
                    to_relay(g, route, sem).start()

    def to_next(g):
        @pl.when(first & has_next & no(leaves(1)))
        def _():
            pass_slot(g, 3, 1, 2, 0).start()

        @pl.when(second & has_next & no(leaves(2)))
        def _():
            pass_slot(g, 3, 2, 1, 0).start()

        cross(g, (1, 2), 0)

        @pl.when(first)
        def _():
            to_sibling(g).start()

    def next_left(g):
        @pl.when(has_next)
        def _():
            pass_slot(g, 3, 1, 1, 0).wait_send()

    def ahead_second(g):
        @pl.when(second & has_second)
        def _():
            to_second(g).start()
        cross(g, (0,), 1)

    def second_left(g):
        @pl.when(second & sends_second)
        def _():
            to_second(g).wait_send()

    def relay(g):
        for route in relays:
            @pl.when(seq == route[3])
            def _():
                to_relay(g, route, 0).wait_recv()
                for copy in from_relay(g, route):
                    copy.start()

    def relay_second(g):
        @pl.when(passes)
        def _():
            to_second(g).wait_recv()
            from_second(g).start()

    def pass_on(g):
        @pl.when(chip >= 1)
        def _():
            arrived(g, 2)
        pass_slot(g, 2, 1, 1, 2).start()

        @pl.when(chip >= 1)
        def _():
            arrived(g, 1)
        pass_slot(g, 1, 0, 1, 3).start()

    def window_in(g):
        @pl.when(first & (chip >= 2))
        def _():
            arrived(g, 0)

        @pl.when(second)
        def _():
            for i in range(3):
                arrived(g, i)

    for copy in own:
        copy.wait()

    to_next(0)
    ahead_second(0)

    @pl.when(first & (chip == 0))
    def _():
        for ref in kv_refs:
            ref[0:3 * block, :] = jnp.zeros((3 * block, 2 * HEAD), jnp.bfloat16)

    @pl.when(first & (chip == 1))
    def _():
        for ref in kv_refs:
            ref[0:block, :] = jnp.zeros((block, 2 * HEAD), jnp.bfloat16)

    for copy in later:
        copy.wait()
    position = seq * block + lax.broadcasted_iota(jnp.int32, (block, HEAD), 0)
    start_ref[...] = jnp.zeros((block, HEAD), jnp.int32)

    def add_episode(e, end):
        end = end + lengths_ref[e]
        start_ref[...] = jnp.where(position >= end, end, start_ref[...])
        return end

    lax.fori_loop(0, episodes, add_episode, jnp.int32(0))

    def out_columns(k, g, piece):
        return pl.ds(pl.multiple_of(((k * 2 + g) * GROUP + piece * STACK) * HEAD, HEAD), wide)

    def staged(u, piece):
        return stage_ref.at[u, :, pl.ds(piece * wide, wide)]

    def out_copy(u, g, piece, to, source):
        return pltpu.make_async_remote_copy(
            src_ref=staged(u, piece), dst_ref=out_ref.at[:, out_columns(source, g, piece)],
            send_sem=out_send.at[u, piece], recv_sem=out_recv.at[g, source, piece],
            device_id=(seq, to), device_id_type=MESH,
        )

    def aside_copy(u, piece, to, low):
        return pltpu.make_async_remote_copy(
            src_ref=staged(u, piece), dst_ref=carry_ref.at[low, piece],
            send_sem=out_send.at[u, piece], recv_sem=carry_recv.at[low, piece],
            device_id=(seq + aside, to), device_id_type=MESH,
        )

    def carried_copy(low, piece):
        source = (3 - kvh) // 3 * 2 + low
        return pltpu.make_async_remote_copy(
            src_ref=carry_ref.at[low, piece], dst_ref=out_ref.at[:, out_columns(source, 1, piece)],
            send_sem=carry_send.at[low, piece], recv_sem=out_recv.at[1, source, piece],
            device_id=(seq - aside, kvh), device_id_type=MESH,
        )

    def own_copy(u, g, piece):
        return pltpu.make_async_copy(
            staged(u, piece), out_ref.at[:, out_columns(kvh, g, piece)], own_sem.at[g, piece]
        )

    def target(step):
        late, odd = step // 2, step % 2
        upper, low = kvh // 2, kvh % 2
        far = (1 - upper) * (3 - odd) + upper * odd
        near = 2 * upper + (1 - low) * (1 - odd) + low * odd
        return (1 - late) * far + late * near

    def unit(g, step):
        r = target(step)
        u = 4 * g + step
        base = pl.multiple_of(r * rows, rows)
        begin = start_ref[pl.ds(base, rows), 0:1] - (seq * block - WINDOW + base)
        q = [q_ref[g, j, pl.ds(base, rows), :] for j in range(GROUP)]

        def finish(piece, outs):
            for j in range(STACK):
                at = (piece * STACK + j) * HEAD
                stage_ref[u, :, at:at + HEAD] = outs[j]

            on_side = leaving & (step == 0) if g == 1 and late else None

            @pl.when(step < 3 if on_side is None else (step < 3) & no(on_side))
            def _():
                out_copy(u, g, piece, r, kvh).start()

            if on_side is not None:
                @pl.when(on_side)
                def _():
                    aside_copy(u, piece, r, kvh % 2).start()

            @pl.when(step == 3)
            def _():
                own_copy(u, g, piece).start()

        attend(q, kv_refs[g], base, begin, scale, finish)

    sources = sorted({route[0] for route in routes})
    early = one_of(seq, sources) if sources else seq < 0

    @pl.when(early)
    def _():
        next_left(0)
        to_next(1)
        second_left(0)
        ahead_second(1)
    relay(0)
    relay_second(0)

    @pl.when(no(early))
    def _():
        next_left(0)
        to_next(1)

    @pl.when(first)
    def _():
        pass_on(0)

    @pl.when(no(early))
    def _():
        second_left(0)
        ahead_second(1)
    window_in(0)

    @pl.loop(0, 4)
    def _(step):
        @pl.when(step == 1)
        def _():
            relay(1)
            relay_second(1)

        @pl.when(first & (step == 2))
        def _():
            pass_on(1)

        unit(0, step)

    window_in(1)

    @pl.loop(0, 4)
    def _(step):
        unit(1, step)

    if late:
        @pl.when(carrying & outer)
        def _():
            for low in range(2):
                for piece in range(pieces):
                    aside_copy(0, piece, kvh, low).wait_recv()
                    carried_copy(low, piece).start()
            for low in range(2):
                for piece in range(pieces):
                    carried_copy(low, piece).wait_send()

    next_left(1)
    second_left(1)
    for g in range(2):
        @pl.when(first)
        def _():
            for sem in range(1, 4):
                pass_slot(g, 3, 2, 1, sem).wait_send()

        @pl.when(passes)
        def _():
            from_second(g).wait_send()
        for route in relays:
            @pl.when(seq == route[3])
            def _():
                for copy in from_relay(g, route):
                    copy.wait_send()

    for g in range(2):
        for piece in range(pieces):
            for step in range(3):
                out_copy(4 * g + step, g, piece, kvh, kvh).wait_send()
            own_copy(4 * g + 3, g, piece).wait()
            for step in range(1, n_kvh):
                source = lax.rem(kvh + step, n_kvh)
                out_copy(0, g, piece, source, source).wait_recv()


def body(n_chips, n_kvh, queries, keys, values, episode_lengths):
    block = keys.shape[0]
    rows = block // n_kvh
    width = queries.shape[1]
    hbm = pl.BlockSpec(memory_space=pltpu.HBM)
    return pl.pallas_call(
        functools.partial(kernel, n_chips, n_kvh),
        out_shape=pltpu.VMEM((rows, width * n_kvh), jnp.bfloat16),
        in_specs=[hbm, hbm, hbm, hbm],
        out_specs=pl.BlockSpec(memory_space=pl.ANY),
        scratch_shapes=[
            pltpu.SMEM(episode_lengths.shape, jnp.int32),
            pltpu.VMEM((2, GROUP, block, HEAD), jnp.bfloat16),
            pltpu.VMEM((4 * block, 2 * HEAD), jnp.bfloat16),
            pltpu.VMEM((4 * block, 2 * HEAD), jnp.bfloat16),
            pltpu.VMEM((2, block // 2, 2 * HEAD), jnp.bfloat16),
            pltpu.VMEM((2, block, 2 * HEAD), jnp.bfloat16),
            pltpu.VMEM((2, GROUP // STACK, rows, STACK * HEAD), jnp.bfloat16),
            pltpu.VMEM((block, HEAD), jnp.int32),
            pltpu.VMEM((8, rows, GROUP * HEAD), jnp.bfloat16),
            pltpu.SemaphoreType.DMA((13,)),
            pltpu.SemaphoreType.DMA((2, 5)),
            pltpu.SemaphoreType.DMA((2, 3)),
            pltpu.SemaphoreType.DMA((2,)),
            pltpu.SemaphoreType.DMA((2,)),
            pltpu.SemaphoreType.DMA((2, GROUP // STACK)),
            pltpu.SemaphoreType.DMA((2, GROUP // STACK)),
            pltpu.SemaphoreType.DMA((8, GROUP // STACK)),
            pltpu.SemaphoreType.DMA((2, n_kvh, GROUP // STACK)),
            pltpu.SemaphoreType.DMA((2, GROUP // STACK)),
        ],
        compiler_params=pltpu.CompilerParams(
            collective_id=0, has_side_effects=True, vmem_limit_bytes=40 << 20
        ),
        name="attention",
    )(*(
        pltpu.with_memory_space_constraint(x, pltpu.HBM)
        for x in (episode_lengths, queries, keys, values)
    ))


def solution(mesh):
    return jax.shard_map(
        functools.partial(body, mesh.shape["seq"] // 2, mesh.shape["kvh"]),
        mesh=mesh,
        in_specs=(P("seq", "kvh"), P("seq", "kvh"), P("seq", "kvh"), P()),
        out_specs=P(("seq", "kvh"), None),
        check_vma=False,
    )
```
